128 devices in a mesh: ctx: 8 (over z, core), hr: 16 (over x, y).
Axes of the slice: x: 4, y: 4, z: 4, core: 2. Of those that a mesh axis runs over, the one named last changes fastest.
Arguments:
- token_ids: int32 [2, 8192], P(None, 'ctx'), may hold values from 0 to 32767
- embed_table: bfloat16 [32768, 4096], P(None, 'hr'), may hold values from -6 to 6
- norm_gain: bfloat16 [4096], replicated, may hold values from 0.5 to 1.5
- w_qkv: bfloat16 [4096, 16, 1, 512], P(None, 'hr'), may hold values from -0.09375 to 0.09375
- w_gate: bfloat16 [4096, 2, 8], replicated, may hold values from -0.09375 to 0.09375
- gate_bias: float32 [2, 8], replicated, may hold values from -3 to 110
- head_gain: bfloat16 [8, 512], replicated, may hold values from 0.099609375 to 1.8984375
- w_out: bfloat16 [4096, 4096], P(None, 'hr'), may hold values from -0.09375 to 0.09375
- owner: int32 [16], replicated, may hold values from 0 to 7, as said below
Outputs:
- block_out: bfloat16 [2, 8192, 4096], P(None, 'ctx', 'hr')
- memory_c: float32 [8, 16, 1, 256, 512], P('ctx', 'hr')
- memory_n: float32 [8, 16, 1, 256], P('ctx', 'hr')
- memory_m: float32 [8, 16, 1], P('ctx', 'hr')
The draws below stay inside these ranges and needn't reach their ends.
Inputs may be any that keep to these rules, and one draw needn't show every extreme that they name: `owner`: every index along ctx owns the same number of memory groups.
All inputs are finite; a program needn't handle non-finite values.
Results may differ from the reference program's by a relative error of at most 0.01.
Values may be sent and summed in bfloat16 or wider, within the bound.
A program may use at most 128 MiB of HBM per device.

```python
import math
import jax
import jax.numpy as jnp
import numpy as np
from jax import lax

D = 4096
NH = 8
DK = 256
DV = 512
VOC = 32768
REQ = 2
SLAB = 8192
HPD = 1
BLK = 512
N_CTX = 8


def draw_gate_bias(key, part):
    key = jax.random.fold_in(key, 11)
    key_keep, key_input = jax.random.split(key, 2)
    keep = jnp.exp(jax.random.uniform(key_keep, (NH,), jnp.float32, math.log(30.0), math.log(4.0 * SLAB)))
    inputs = jax.random.uniform(key_input, (NH,), jnp.float32, -3.0, 3.0)
    return jnp.stack([inputs, jnp.log(keep)]).astype(jnp.float32)


def draw_owner(key, part):
    key = jax.random.fold_in(key, 23)
    group_count = 2 * NH // HPD
    tiled = jnp.arange(group_count, dtype=jnp.int32) % N_CTX
    return jax.random.permutation(key, tiled).astype(jnp.int32)


def with_ends(drawn, stream_key, low, high):
    dims = drawn.shape
    index_at = [jax.random.randint(jax.random.fold_in(stream_key, axis), (), 0, dims[axis]) for axis in range(len(dims))]
    drawn = drawn.at[tuple(index_at)].set(low)
    longest = dims.index(max(dims))
    index_at[longest] = (index_at[longest] + 1) % dims[longest]
    return drawn.at[tuple(index_at)].set(high)


def block_scale(stream_key, shape, cuts, low, high):
    gain, own = 1.0, jax.random.fold_in(stream_key, 6)
    for axis_at, blocks in cuts:
        draws = jnp.exp(jax.random.uniform(jax.random.fold_in(own, axis_at), (blocks,), jnp.float32, low / len(cuts), high / len(cuts)))
        gain = gain * jnp.repeat(draws, shape[axis_at] // blocks).reshape([-1 if axis == axis_at else 1 for axis in range(len(shape))])
    return gain


def cumulative_ranks(count, slope):
    portions = [(1 << 20) // math.isqrt(grade ** slope) + 1 for grade in range(1, count + 1)]
    scale = 1 + sum(portions) // (1 << 30)
    return np.cumsum(np.array([max(1, weight // scale) for weight in portions]))


def skewed_ids(stream_key, shape, amount, skew):
    grid = cumulative_ranks(amount, skew)
    ticket = jax.random.randint(jax.random.fold_in(stream_key, 1), shape, 0, int(grid[amount - 1]))
    standing = jnp.searchsorted(jnp.asarray(grid, jnp.int32), ticket, side="right")
    return jax.random.permutation(jax.random.fold_in(stream_key, 2), amount)[standing].astype(jnp.int32)


def scatter_about(key, extent, deviation, limit, cuts=(), kind=jnp.bfloat16):
    values = jax.random.normal(key, extent, jnp.float32) * deviation
    if len(cuts) > 0:
        values = block_scale(key, extent, cuts, -0.22, 0.18) * values
    return jnp.clip(values, min=-limit, max=limit).astype(kind)


def setup_inputs(seed: int = 0) -> dict:
    key_list = jax.random.split(jax.random.key(seed), 10)
    token_ids = with_ends(skewed_ids(key_list[0], (REQ, SLAB), VOC, 2), jax.random.fold_in(key_list[0], 3), 0, VOC - 1).astype(jnp.int32)
    embed_table = scatter_about(key_list[1], (VOC, D), 1.0, 6.0, ((1, 16),))
    norm_gain = jnp.clip(1.0 + 0.1 * jax.random.normal(key_list[2], (D,), jnp.float32), 0.5, 1.5).astype(jnp.bfloat16)
    w_qkv = scatter_about(key_list[3], (D, 2 * NH // HPD, HPD, 2 * DK), D ** -0.5, 0.09375, ((1, 16),))
    w_gate = scatter_about(key_list[4], (D, 2, NH), D ** -0.5, 0.09375)
    gate_bias = draw_gate_bias(jax.random.fold_in(key_list[9], 71), 0)
    head_gain = jnp.clip(1.0 + 0.18 * jax.random.normal(key_list[6], (NH, DV), jnp.float32), 0.099609375, 1.8984375).astype(jnp.bfloat16)
    w_out = scatter_about(key_list[7], (NH * DV, D), (NH * DV) ** -0.5, 0.09375, ((1, 16),))
    owner = draw_owner(jax.random.fold_in(key_list[9], 71), 0)
    return dict(token_ids=token_ids, embed_table=embed_table, norm_gain=norm_gain, w_qkv=w_qkv, w_gate=w_gate, gate_bias=gate_bias, head_gain=head_gain, w_out=w_out, owner=owner)


very_negative = -1e+30
epsilon = 1e-06

def combine(earlier, later):
    decay_one, max_one, memory_one, norm_one = earlier
    decay_two, max_two, memory_two, norm_two = later
    joined = jnp.maximum(decay_two + max_one, max_two)
    first_w = jnp.exp(decay_two + max_one - joined)
    second_w = jnp.exp(max_two - joined)
    memory = first_w[..., None, None] * memory_one + second_w[..., None, None] * memory_two
    normer = first_w[..., None] * norm_one + second_w[..., None] * norm_two
    return (decay_one + decay_two, joined, memory, normer)

def block_pass(queries, key_rows, values, in_gate, log_forget):
    length = queries.shape[0]
    inv_root = 1.0 / math.sqrt(queries.shape[1])
    cumulative = jnp.cumsum(log_forget)
    total_decay = cumulative[-1]
    causal_mask = lax.broadcasted_iota(jnp.int32, (length, length), 0) >= lax.broadcasted_iota(jnp.int32, (length, length), 1)
    exponent = jnp.where(causal_mask, cumulative[:, None] - cumulative[None, :] + in_gate[None, :], very_negative)
    local_max = lax.optimization_barrier(jnp.max(exponent, axis=1))
    weights = jnp.exp(exponent - local_max[:, None])
    scores = jnp.dot(queries, key_rows.T, preferred_element_type=jnp.float32) * inv_root
    weighted = weights * scores
    numerator = jnp.dot(weighted.astype(jnp.bfloat16), values, preferred_element_type=jnp.float32)
    denominator = lax.optimization_barrier(jnp.sum(weighted, axis=1))
    tail_decay = total_decay - cumulative + in_gate
    block_max = jnp.max(tail_decay)
    scaled_keys = key_rows.astype(jnp.float32) * jnp.exp(tail_decay - block_max)[:, None]
    block_memory = jnp.dot(scaled_keys.astype(jnp.bfloat16).T, values, preferred_element_type=jnp.float32)
    block_norm = lax.optimization_barrier(jnp.sum(scaled_keys, axis=0))
    return (numerator, denominator, local_max, cumulative, (total_decay, block_max, block_memory, block_norm))

def finish(numerator, denominator, local_max, cumulative, state, queries):
    decay_in, max_in, memory_in, norm_in = state
    inv_root = 1.0 / math.sqrt(queries.shape[1])
    row_max = jnp.maximum(cumulative + max_in, local_max)
    inner = jnp.exp(local_max - row_max)
    outer = jnp.exp(cumulative + max_in - row_max)
    scaled_q = queries.astype(jnp.float32) * inv_root
    carried = jnp.dot(queries, memory_in.astype(jnp.bfloat16), preferred_element_type=jnp.float32) * inv_root
    top = inner[:, None] * numerator + outer[:, None] * carried
    bottom = inner * denominator + outer * jnp.dot(scaled_q, norm_in, precision=lax.Precision.HIGHEST)
    return top / jnp.maximum(jnp.abs(bottom), jnp.exp(-row_max))[:, None]

def reference(token_ids, embed_table, norm_gain, w_qkv, w_gate, gate_bias, head_gain, w_out, owner):
    groups = 2 * NH // HPD
    blocks = SLAB // BLK
    embedded = embed_table[token_ids]
    wide = embedded.astype(jnp.float32)
    normed = (wide * lax.rsqrt(lax.optimization_barrier(jnp.mean(wide * wide, axis=-1, keepdims=True)) + epsilon) * norm_gain.astype(jnp.float32)).astype(jnp.bfloat16)
    flat = normed.reshape(REQ * SLAB, D)
    split_w = w_qkv.reshape(D, NH // HPD, 2, HPD, 2 * DK)
    w_pair = split_w[:, :, 0].reshape(D, NH * 2 * DK)
    w_value = split_w[:, :, 1].reshape(D, NH * DV)
    pair_proj = jnp.dot(flat, w_pair, preferred_element_type=jnp.float32).astype(jnp.bfloat16).reshape(REQ, SLAB, NH, 2 * DK)
    value_proj = jnp.dot(flat, w_value, preferred_element_type=jnp.float32).astype(jnp.bfloat16).reshape(REQ, SLAB, NH, DV)
    gate_pre = jnp.dot(flat, w_gate.reshape(D, 2 * NH), preferred_element_type=jnp.float32).reshape(REQ, SLAB, 2, NH) + gate_bias
    in_gate = gate_pre[:, :, 0]
    log_forget = jax.nn.log_sigmoid(gate_pre[:, :, 1])

    def by_pair(array, tail):
        return jnp.moveaxis(array, 2, 1).reshape((REQ * NH, SLAB) + tail)
    queries_all = by_pair(pair_proj[..., :DK], (DK,))
    keys_all = by_pair(pair_proj[..., DK:], (DK,))
    values_all = by_pair(value_proj, (DV,))
    gates_in_all = by_pair(in_gate, ())
    gates_forget_all = by_pair(log_forget, ())

    def one_pair(item):
        queries, key_rows, values, gate_in, gate_forget = item
        shaped = (queries.reshape(blocks, BLK, DK), key_rows.reshape(blocks, BLK, DK), values.reshape(blocks, BLK, DV), gate_in.reshape(blocks, BLK), gate_forget.reshape(blocks, BLK))

        def advance(state, block):
            q_block, k_block, v_block, i_block, f_block = block
            numerator, denominator, local_max, cumulative, summary = block_pass(q_block, k_block, v_block, i_block, f_block)
            hidden_block = finish(numerator, denominator, local_max, cumulative, state, q_block)
            return (combine(state, summary), hidden_block)
        start = (jnp.float32(0.0), jnp.float32(very_negative), jnp.zeros((DK, DV), jnp.float32), jnp.zeros((DK,), jnp.float32))
        final, hidden_blocks = lax.scan(advance, start, shaped)
        return (hidden_blocks.reshape(SLAB, DV), final)
    hidden, finals = lax.map(one_pair, (queries_all, keys_all, values_all, gates_in_all, gates_forget_all))
    hidden = hidden.reshape(REQ, NH, SLAB, DV)
    head_normed = (hidden * lax.rsqrt(lax.optimization_barrier(jnp.mean(hidden * hidden, axis=-1, keepdims=True)) + epsilon) * head_gain.astype(jnp.float32)[None, :, None, :]).astype(jnp.bfloat16)
    joined = jnp.moveaxis(head_normed, 1, 2).reshape(REQ * SLAB, NH * DV)
    mixed = jnp.dot(joined, w_out, preferred_element_type=jnp.float32).reshape(REQ, SLAB, D)
    block_out = (wide + mixed).astype(jnp.bfloat16)

    def arrange(values, tail):
        shaped = values.reshape((REQ, NH // HPD, HPD) + tail)
        return jnp.moveaxis(shaped, 0, 1).reshape((groups, HPD) + tail)
    slots = jnp.arange(N_CTX, dtype=jnp.int32)[:, None]
    chosen = (owner.astype(jnp.int32)[None, :] == slots).astype(jnp.float32)
    memory_c = chosen[:, :, None, None, None] * arrange(finals[2], (DK, DV))[None]
    memory_n = chosen[:, :, None, None] * arrange(finals[3], (DK,))[None]
    memory_m = chosen[:, :, None] * arrange(finals[1], ())[None]
    return (block_out, memory_c, memory_n, memory_m)
```

```python
import jax
import jax.numpy as jnp
from jax import lax
from jax.experimental import pallas as pl
from jax.experimental.pallas import tpu as pltpu
from jax.sharding import PartitionSpec as P

MESH = pl.DeviceIdType.MESH
F32 = jnp.float32
BF16 = jnp.bfloat16
very_negative = -1e30
epsilon = 1e-06

WIDTH = 4096
ROWS = 1024
HALF = 512
PIECES = 2
PIECE = HALF // PIECES
KEY = 256
VAL = 512
SENDS = 96


def dot(a, b):
    return jnp.dot(a, b, preferred_element_type=F32)


def kernel(
    emb,
    w_own,
    w_out,
    w_gate,
    bias,
    gain,
    out_rows,
    out_mem,
    out_aux,
    xb,
    wb,
    wo,
    qs,
    ks,
    vs,
    gs,
    num,
    den,
    rows_in,
    cols_in,
    sum_c,
    sum_aux,
    state_c,
    hn,
    act,
    opp,
    right_p,
    left_p,
    own_p,
    opp_in,
    right_in,
    left_in,
    total,
    mem_out,
    aux_out,
    send_sem,
    local_sem,
    sem_a,
    sem_ring,
    sem_sib,
    sem_w,
    sem_wz,
    sem_wo,
    sem_woz,
    sem_state,
    sem_hn,
    sem_red,
    sem_out,
    sem_mem,
):
    c = lax.axis_index("ctx")
    h = lax.axis_index("hr")
    x, y = h // 4, h % 4
    z, k = c // 2, c % 2
    req, par = y // 2, y % 2

    def dev(x_, y_, z_, k_):
        return (z_ * 2 + k_, x_ * 4 + y_)

    def rel(base, step):
        return lax.rem(base + step, 4)

    sib = dev(x, y, z, 1 - k)
    x_next, x_prev = dev(rel(x, 1), y, z, k), dev(rel(x, 3), y, z, k)
    z_next, z_prev = dev(x, y, rel(z, 1), k), dev(x, y, rel(z, 3), k)
    y_mate = 2 * req + 1 - par

    partners = [sib]
    for step in (1, 2, 3):
        for core in (0, 1):
            partners.append(dev(x, rel(y, step), z, core))
        partners.append(dev(rel(x, step), y, z, k))
        partners.append(dev(x, y, rel(z, step), k))
        partners.append(dev(x, y_mate, rel(z, step), k))
    barrier = pltpu.get_barrier_semaphore()
    for partner in partners:
        pl.semaphore_signal(barrier, inc=1, device_id=partner, device_id_type=MESH)
    pl.semaphore_wait(barrier, len(partners))

    pending = []

    def push(src, dst, sem, target, when=None):
        slot = len(pending)
        copy = pltpu.make_async_remote_copy(
            src_ref=src,
            dst_ref=dst,
            send_sem=send_sem.at[slot],
            recv_sem=sem,
            device_id=target,
            device_id_type=MESH,
        )
        pending.append((copy, when))
        if when is None:
            copy.start()
        else:
            pl.when(when)(copy.start)

    def here(src, dst, sem, when):
        copy = pltpu.make_async_copy(src, dst, sem)
        pl.when(when)(copy.start)

    def arrived(dst, sem):
        pltpu.make_async_remote_copy(
            src_ref=dst,
            dst_ref=dst,
            send_sem=send_sem.at[0],
            recv_sem=sem,
            device_id=sib,
            device_id_type=MESH,
        ).wait_recv()

    k_half = k * HALF

    for piece in range(PIECES):
        for r_ in (0, 1):
            for kd in (0, 1):
                y_to = 2 * r_ + k
                mine = (y_to == y) & (kd == k)
                start = kd * HALF + piece * PIECE
                src = emb.at[r_, pl.ds(start, PIECE), :]
                dst = xb.at[x, pl.ds(start, PIECE), pl.ds(pl.multiple_of(y * 256, 256), 256)]
                push(src, dst, sem_a.at[piece, y], dev(x, y_to, z, kd), jnp.logical_not(mine))
                here(src, dst, sem_a.at[piece, y], mine)

    w_rows = pl.ds(pl.multiple_of(z * 1024 + k * 512, 512), 512)
    for step in (1, 3, 2):
        push(
            w_own.at[w_rows, :],
            wb.at[y % 2, w_rows, :],
            sem_w.at[y % 2, k],
            dev(x, rel(y, step), z, y // 2),
        )
    w_local = pltpu.make_async_copy(w_own, wb.at[y % 2], local_sem.at[0])
    pl.when(k == y // 2)(w_local.start)

    o_rows = pl.multiple_of(z * 256 + k * 128, 128)
    for step in (1, 3, 2):
        x_to = rel(x, step)
        push(
            w_out.at[pl.ds(pl.multiple_of(x_to * 1024 + o_rows, 128), 128), :],
            wo.at[y, pl.ds(o_rows, 128), pl.ds(pl.multiple_of(x * 256, 256), 256)],
            sem_wo.at[x],
            dev(x_to, y, z, k),
        )
    o_local = pltpu.make_async_copy(
        w_out.at[pl.ds(pl.multiple_of(x * 1024 + o_rows, 128), 128), :],
        wo.at[y, pl.ds(o_rows, 128), pl.ds(pl.multiple_of(x * 256, 256), 256)],
        local_sem.at[1],
    )
    o_local.start()

    def rows_of(block, core, piece, half=None):
        if half is None:
            return xb.at[block, pl.ds(core * HALF + piece * PIECE, PIECE), :]
        return xb.at[
            block, pl.ds(core * HALF + piece * PIECE + half * (PIECE // 2), PIECE // 2), :
        ]

    xl, xr, xo = rel(x, 3), rel(x, 1), rel(x, 2)
    for piece in range(PIECES):
        for y_ in range(4):
            arrived(
                xb.at[x, pl.ds(k_half + piece * PIECE, PIECE), pl.ds(y_ * 256, 256)],
                sem_a.at[piece, y_],
            )
        block = rows_of(x, k, piece)
        push(block, block, sem_ring.at[0, piece], x_next)
        push(block, block, sem_ring.at[1, piece], x_prev)
        push(block, block, sem_sib.at[0, piece], sib)

    foreign = [(2 * k + j) != y for j in (0, 1)]

    def w_part(j, plane, part):
        return wb.at[j, pl.ds(pl.multiple_of(plane * 1024 + part * 512, 512), 512), :]

    zl, zr, zo = rel(z, 3), rel(z, 1), rel(z, 2)
    for j in (0, 1):
        for part in (0, 1):
            block = w_part(j, z, part)

            @pl.when(foreign[j])
            def _(block=block, j=j, part=part):
                arrived(block, sem_w.at[j, part])

            push(block, block, sem_wz.at[0, j, part], z_next, foreign[j])
            push(block, block, sem_wz.at[1, j, part], z_prev, foreign[j])

    for x_ in (1, 2, 3):
        src_x = rel(x, x_)
        arrived(
            wo.at[y, pl.ds(o_rows, 128), pl.ds(pl.multiple_of(src_x * 256, 256), 256)],
            sem_wo.at[src_x],
        )
    o_local.wait()
    block = wo.at[y, pl.ds(o_rows, 128), :]
    for step in (1, 3, 2):
        push(block, block, sem_wo.at[4 + y], dev(x, rel(y, step), z, k))

    for piece in range(PIECES):
        block = rows_of(xl, k, piece)
        arrived(block, sem_ring.at[0, piece])
        half = rows_of(xl, k, piece, 0)
        push(half, half, sem_ring.at[2, piece], x_next)
        push(block, block, sem_sib.at[1, piece], sib)
        block = rows_of(xr, k, piece)
        arrived(block, sem_ring.at[1, piece])
        half = rows_of(xr, k, piece, 1)
        push(half, half, sem_ring.at[3, piece], x_prev)
        push(block, block, sem_sib.at[2, piece], sib)

    for j in (0, 1):
        for part in (0, 1):
            from_left, from_right = w_part(j, zl, part), w_part(j, zr, part)

            @pl.when(foreign[j])
            def _(from_left=from_left, from_right=from_right, j=j, part=part):
                arrived(from_left, sem_wz.at[0, j, part])
                arrived(from_right, sem_wz.at[1, j, part])

            if part == 0:
                push(from_left, from_left, sem_wz.at[2, j, 0], z_next, foreign[j])
            else:
                push(from_right, from_right, sem_wz.at[2, j, 1], z_prev, foreign[j])

    for piece in range(PIECES):
        block = rows_of(xo, k, piece)
        for half in (0, 1):
            arrived(rows_of(xo, k, piece, half), sem_ring.at[2 + half, piece])
        push(block, block, sem_sib.at[3, piece], sib)

    for step in (1, 2, 3):
        y_ = rel(y, step)
        arrived(wo.at[y_, pl.ds(o_rows, 128), :], sem_wo.at[4 + y_])

    def o_part(plane, core, half=None):
        if half is None:
            return wo.at[:, pl.ds(pl.multiple_of(plane * 256 + core * 128, 128), 128), :]
        return wo.at[:, pl.ds(pl.multiple_of(plane * 256 + core * 128 + half * 64, 64), 64), :]

    for index, block_x in enumerate((x, xl, xr, xo)):
        for piece in range(PIECES):
            arrived(rows_of(block_x, 1 - k, piece), sem_sib.at[index, piece])
    pl.when(k == y // 2)(w_local.wait)
    for j in (0, 1):
        for part in (0, 1):
            block = w_part(j, zo, part)

            @pl.when(foreign[j])
            def _(block=block, j=j, part=part):
                arrived(block, sem_wz.at[2, j, part])

    block = o_part(z, k)
    push(block, block, sem_woz.at[0], z_next)
    push(block, block, sem_woz.at[1], z_prev)
    push(block, block, sem_woz.at[4], sib)

    tile = 256

    def project(step, carry):
        rows = pl.ds(pl.multiple_of(step * tile, tile), tile)
        squares = jnp.zeros((tile, 1), F32)
        accs = [jnp.zeros((tile, 512), F32), jnp.zeros((tile, 512), F32)]
        gate = jnp.zeros((tile, 128), F32)
        for block in range(4):
            a = xb[block, rows, :]
            wide = a.astype(F32)
            squares += jnp.sum(wide * wide, axis=1, keepdims=True)
            depth = slice(block * 1024, block * 1024 + 1024)
            for j in (0, 1):
                accs[j] = accs[j] + dot(a, wb[j, depth, :])
            gate = gate + dot(a, w_gate[depth, :])
        scale = lax.rsqrt(squares / WIDTH + epsilon)
        qk = (accs[0] * scale).astype(BF16)
        qs[rows, :] = qk[:, :KEY]
        ks[rows, :] = qk[:, KEY:]
        vs[rows, :] = (accs[1] * scale).astype(BF16)
        gs[rows, :] = gate * scale + bias[0:1, :]
        return carry

    lax.fori_loop(0, ROWS // tile, project, 0)

    head = 2 * x + k
    gates_t = gs[...].T
    sub = lax.broadcasted_iota(jnp.int32, (128, ROWS), 0)
    gate_in = jnp.sum(jnp.where(sub == head, gates_t, 0.0), axis=0, keepdims=True)
    pre_forget = jnp.sum(jnp.where(sub == head + 8, gates_t, 0.0), axis=0, keepdims=True)
    gate_in = jnp.broadcast_to(gate_in, (8, ROWS))
    pre_forget = jnp.broadcast_to(pre_forget, (8, ROWS))
    log_forget = jnp.minimum(pre_forget, 0.0) - jnp.log1p(jnp.exp(-jnp.abs(pre_forget)))
    lane = lax.broadcasted_iota(jnp.int32, (8, ROWS), 1)
    cum = log_forget
    step = 1
    while step < ROWS:
        cum = cum + jnp.where(lane >= step, pltpu.roll(cum, step, 1), 0.0)
        step *= 2
    lead = gate_in - cum
    peak = lead
    step = 1
    while step < ROWS:
        peak = jnp.maximum(peak, jnp.where(lane >= step, pltpu.roll(peak, step, 1), very_negative))
        step *= 2
    rows_in[0:8, :] = cum
    rows_in[8:16, :] = lead
    rows_in[16:24, :] = peak
    last_peak = jnp.max(lead, axis=1, keepdims=True)[0:1, :]
    decay = jnp.sum(jnp.where(lane == ROWS - 1, cum, 0.0), axis=1, keepdims=True)[0:1, :]
    rows_in[24:32, :] = jnp.exp(lead - last_peak)
    rows_in[32:, :] = jnp.zeros((96, ROWS), F32)
    cols_in[...] = rows_in[...].T

    scaled = ks[...].astype(F32) * cols_in[:, 24:25]
    norm_sum = jnp.sum(scaled, axis=0, keepdims=True)
    memory = lax.dot_general(
        scaled.astype(BF16), vs[...], (((0,), (0,)), ((), ())), preferred_element_type=F32
    )
    chunk = 2 * z + par
    sum_c[chunk] = memory.astype(BF16)
    row = lax.broadcasted_iota(jnp.int32, (8, KEY), 0)
    aux = jnp.where(row == 0, norm_sum, jnp.where(row == 1, decay + last_peak, decay))
    sum_aux[chunk] = aux
    peers = [dev(x, y_mate, z, k)]
    chunks = [2 * z + 1 - par]
    for step in (1, 3, 2):
        peers += [dev(x, y, rel(z, step), k), dev(x, y_mate, rel(z, step), k)]
        chunks += [2 * rel(z, step) + par, 2 * rel(z, step) + 1 - par]
    for peer in peers:
        push(sum_aux.at[chunk], sum_aux.at[chunk], sem_state.at[0, chunk], peer)
        push(sum_c.at[chunk], sum_c.at[chunk], sem_state.at[1, chunk], peer)

    lead_row = rows_in[8:9, :]
    for index in range(ROWS // tile):
        rows = slice(index * tile, (index + 1) * tile)
        seen = (index + 1) * tile
        scores = lax.dot_general(
            qs[rows, :], ks[:seen, :], (((1,), (1,)), ((), ())), preferred_element_type=F32
        )
        t_at = lax.broadcasted_iota(jnp.int32, (tile, seen), 0) + index * tile
        s_at = lax.broadcasted_iota(jnp.int32, (tile, seen), 1)
        exponent = jnp.where(t_at >= s_at, lead_row[:, :seen] - cols_in[rows, 16:17], very_negative)
        weighted = jnp.exp(exponent) * (scores * 0.0625)
        num[rows, :] = dot(weighted.astype(BF16), vs[:seen, :])
        den[rows, :] = jnp.broadcast_to(jnp.sum(weighted, axis=1, keepdims=True), (tile, 128))

    block = o_part(zl, k)
    arrived(block, sem_woz.at[0])
    half = o_part(zl, k, 0)
    push(half, half, sem_woz.at[2], z_next)
    push(block, block, sem_woz.at[5], sib)
    block = o_part(zr, k)
    arrived(block, sem_woz.at[1])
    half = o_part(zr, k, 1)
    push(half, half, sem_woz.at[3], z_prev)
    push(block, block, sem_woz.at[6], sib)

    for chunk_ in chunks:
        arrived(sum_aux.at[chunk_], sem_state.at[0, chunk_])
        arrived(sum_c.at[chunk_], sem_state.at[1, chunk_])

    def combined(limit):
        state_c[...] = jnp.zeros_like(state_c)

        def body(at, state):
            top, norm = state
            here_ = sum_aux[at]
            peak_, decay_ = here_[1:2, :], here_[2:3, :]
            joined = jnp.maximum(decay_ + top, peak_)
            one, two = jnp.exp(decay_ + top - joined), jnp.exp(peak_ - joined)
            state_c[...] = (
                jnp.concatenate([one, one], axis=1) * state_c[...]
                + jnp.concatenate([two, two], axis=1) * sum_c[at].astype(F32)
            )
            return joined, one * norm + two * here_[0:1, :]

        return lax.fori_loop(
            0,
            limit,
            body,
            (jnp.full((1, KEY), very_negative, F32), jnp.zeros((1, KEY), F32)),
        )

    top_in, norm_in = combined(chunk)
    hn_gain = gain[pl.ds(head, 1), :]
    memory_in = state_c[...].astype(BF16)
    for index in range(ROWS // tile):
        rows = slice(index * tile, (index + 1) * tile)
        q = qs[rows, :]
        carried = dot(q, memory_in) * 0.0625
        carried_norm = jnp.sum(q.astype(F32) * norm_in, axis=1, keepdims=True) * 0.0625
        here_max = cols_in[rows, 16:17]
        both = jnp.maximum(top_in[:, 0:1], here_max)
        inner, outer = jnp.exp(here_max - both), jnp.exp(top_in[:, 0:1] - both)
        row_max = cols_in[rows, 0:1] + both
        bottom = inner * den[rows, 0:1] + outer * carried_norm
        divisor = jnp.maximum(jnp.abs(bottom), jnp.exp(-row_max))
        hidden = (inner * num[rows, :] + outer * carried) / divisor
        scale = lax.rsqrt(jnp.mean(hidden * hidden, axis=1, keepdims=True) + epsilon)
        hn[rows, :] = (hidden * scale * hn_gain).astype(BF16)

    other = pl.ds(pl.multiple_of((1 - k) * HALF, HALF), HALF)
    mine_rows = pl.ds(pl.multiple_of(k_half, HALF), HALF)
    push(hn.at[other, :], act.at[k], sem_hn.at[0], sib)
    act[k] = hn[mine_rows, :]
    block = o_part(zo, k)
    arrived(o_part(zo, k, 0), sem_woz.at[2])
    arrived(o_part(zo, k, 1), sem_woz.at[3])
    push(block, block, sem_woz.at[7], sib)
    arrived(act.at[1 - k], sem_hn.at[0])
    for index, plane in enumerate((z, zl, zr, zo)):
        arrived(o_part(plane, 1 - k), sem_woz.at[4 + index])

    def partial(block_x, y_, rows):
        cols = pl.ds(pl.multiple_of(block_x * 256, 256), 256)
        return dot(act[0, rows, :], wo[y_, 0:512, cols]) + dot(
            act[1, rows, :], wo[y_, 512:1024, cols]
        )

    low, high = slice(0, HALF // 2), slice(HALF // 2, HALF)

    def fill(target, block_x, rows, extra=None):
        for y_ in range(4):
            cols = slice(y_ * 256, y_ * 256 + 256)
            value = partial(block_x, y_, rows)
            if extra is not None:
                value = value + extra[:, cols].astype(F32)
            target[rows, cols] = value.astype(target.dtype)

    fill(opp, xo, low)
    push(opp.at[low, :], opp_in.at[0], sem_red.at[0], x_next)
    fill(opp, xo, high)
    push(opp.at[high, :], opp_in.at[1], sem_red.at[1], x_prev)
    fill(right_p, xr, high)
    push(right_p.at[high, :], left_in.at[high, :], sem_red.at[2], x_next)
    fill(left_p, xl, low)
    push(left_p.at[low, :], right_in.at[low, :], sem_red.at[3], x_prev)
    arrived(opp_in.at[0], sem_red.at[0])
    fill(right_p, xr, low, opp_in.at[0])
    push(right_p.at[low, :], left_in.at[low, :], sem_red.at[4], x_next)
    arrived(opp_in.at[1], sem_red.at[1])
    fill(left_p, xl, high, opp_in.at[1])
    push(left_p.at[high, :], right_in.at[high, :], sem_red.at[5], x_prev)
    fill(own_p, x, low)
    fill(own_p, x, high)

    top_end, norm_end = combined(8)
    row = lax.broadcasted_iota(jnp.int32, (8, KEY), 0)
    aux_out[...] = jnp.where(row == 0, norm_end, top_end)
    keep_here = (k == req) & (par == k)
    mem_to = dev(x, 2 * k + req, z, par)
    push(state_c, out_mem, sem_mem.at[0], mem_to, jnp.logical_not(keep_here))
    push(aux_out, out_aux, sem_mem.at[1], mem_to, jnp.logical_not(keep_here))
    here(state_c, out_mem, sem_mem.at[0], keep_here)
    here(aux_out, out_aux, sem_mem.at[1], keep_here)

    for index, rows, sems in ((1, high, (2, 5)), (0, low, (4, 3))):
        arrived(left_in.at[rows, :], sem_red.at[sems[0]])
        arrived(right_in.at[rows, :], sem_red.at[sems[1]])
        total[rows, :] = (
            own_p[rows, :] + left_in[rows, :].astype(F32) + right_in[rows, :].astype(F32)
        ).astype(BF16)
        for y_ in range(4):
            src = total.at[rows, pl.ds(y_ * 256, 256)]
            dst = out_rows.at[
                req, pl.ds(pl.multiple_of(k_half + index * 256, 256), 256), :
            ]
            mine = (y == y_) & (par == k)
            push(
                src, dst, sem_out.at[index, req, k], dev(x, y_, z, par), jnp.logical_not(mine)
            )
            here(src, dst, sem_out.at[index, req, k], mine)

    for index in (1, 0):
        for r_ in (0, 1):
            for k_ in (0, 1):
                arrived(
                    out_rows.at[r_, pl.ds(k_ * HALF + index * 256, 256), :],
                    sem_out.at[index, r_, k_],
                )
    arrived(out_mem, sem_mem.at[0])
    arrived(out_aux, sem_mem.at[1])
    for copy, when in pending:
        if when is None:
            copy.wait_send()
        else:
            pl.when(when)(copy.wait_send)


def local(token_ids, embed_table, norm_gain, w_qkv, w_gate, gate_bias, head_gain, w_out, owner):
    hr_index = lax.axis_index("hr")
    ctx_index = lax.axis_index("ctx")
    embedded = embed_table.at[token_ids].get(mode="promise_in_bounds")
    gain = norm_gain.astype(F32)[:, None]
    w_own = (w_qkv.reshape(WIDTH, 512).astype(F32) * gain).astype(BF16)
    gates = (w_gate.reshape(WIDTH, 16).astype(F32) * gain).astype(BF16)
    gates = jnp.pad(gates, ((0, 0), (0, 112)))
    bias = jnp.broadcast_to(jnp.pad(gate_bias.reshape(1, 16), ((0, 0), (0, 112))), (8, 128))
    vmem = pl.BlockSpec(memory_space=pltpu.VMEM)
    hbm = pl.BlockSpec(memory_space=pl.ANY)
    dma = pltpu.SemaphoreType.DMA
    rows, mem, aux = pl.pallas_call(
        kernel,
        out_shape=(
            jax.ShapeDtypeStruct((2, ROWS, 256), BF16),
            jax.ShapeDtypeStruct((KEY, VAL), F32),
            jax.ShapeDtypeStruct((8, KEY), F32),
        ),
        in_specs=[vmem, hbm, hbm, vmem, vmem, vmem],
        out_specs=(vmem, vmem, vmem),
        scratch_shapes=[
            pltpu.VMEM((4, ROWS, 1024), BF16),
            pltpu.VMEM((2, WIDTH, 512), BF16),
            pltpu.VMEM((4, 1024, 1024), BF16),
            pltpu.VMEM((ROWS, KEY), BF16),
            pltpu.VMEM((ROWS, KEY), BF16),
            pltpu.VMEM((ROWS, VAL), BF16),
            pltpu.VMEM((ROWS, 128), F32),
            pltpu.VMEM((ROWS, VAL), F32),
            pltpu.VMEM((ROWS, 128), F32),
            pltpu.VMEM((128, ROWS), F32),
            pltpu.VMEM((ROWS, 128), F32),
            pltpu.VMEM((8, KEY, VAL), BF16),
            pltpu.VMEM((8, 8, KEY), F32),
            pltpu.VMEM((KEY, VAL), F32),
            pltpu.VMEM((ROWS, VAL), BF16),
            pltpu.VMEM((2, HALF, VAL), BF16),
            pltpu.VMEM((HALF, 1024), BF16),
            pltpu.VMEM((HALF, 1024), BF16),
            pltpu.VMEM((HALF, 1024), BF16),
            pltpu.VMEM((HALF, 1024), F32),
            pltpu.VMEM((2, HALF // 2, 1024), BF16),
            pltpu.VMEM((HALF, 1024), BF16),
            pltpu.VMEM((HALF, 1024), BF16),
            pltpu.VMEM((HALF, 1024), BF16),
            pltpu.VMEM((8, KEY), F32),
            pltpu.VMEM((8, KEY), F32),
            dma((SENDS,)),
            dma((2,)),
            dma((PIECES, 4)),
            dma((4, PIECES)),
            dma((4, PIECES)),
            dma((2, 2)),
            dma((3, 2, 2)),
            dma((8,)),
            dma((8,)),
            dma((2, 8)),
            dma((1,)),
            dma((6,)),
            dma((2, 2, 2)),
            dma((2,)),
        ],
        compiler_params=pltpu.CompilerParams(
            collective_id=0, has_side_effects=True, vmem_limit_bytes=60 * 2**20
        ),
    )(embedded, w_own, w_out, gates, bias, head_gain.astype(F32))
    block_out = (embedded.astype(F32) + rows.astype(F32)).astype(BF16)
    owner_here = lax.dynamic_slice_in_dim(owner, hr_index, 1, 0)[0]
    keep = (owner_here == ctx_index).astype(F32)
    memory_c = (keep * mem)[None, None, None]
    memory_n = (keep * aux[0])[None, None, None]
    memory_m = (keep * aux[1, 0:1])[None, None]
    return (block_out, memory_c, memory_n, memory_m)


def solution(mesh):
    return jax.shard_map(
        local,
        mesh=mesh,
        in_specs=(
            P(None, "ctx"),
            P(None, "hr"),
            P(),
            P(None, "hr", None, None),
            P(),
            P(),
            P(),
            P(None, "hr"),
            P(),
        ),
        out_specs=(
            P(None, "ctx", "hr"),
            P("ctx", "hr", None, None, None),
            P("ctx", "hr", None, None),
            P("ctx", "hr", None),
        ),
        check_vma=False,
    )
```

```python
import jax
import jax.numpy as jnp
from jax import lax
from jax.experimental import pallas as pl
from jax.experimental.pallas import tpu as pltpu
from jax.sharding import PartitionSpec as P

MESH = pl.DeviceIdType.MESH
F32 = jnp.float32
BF16 = jnp.bfloat16
very_negative = -1e30
epsilon = 1e-06

WIDTH = 4096
ROWS = 1024
HALF = 512
PIECES = 2
PIECE = HALF // PIECES
KEY = 256
VAL = 512
SENDS = 128
SPREAD = 320
DIRECT = 768
TILE = 256


def dot(a, b):
    return jnp.dot(a, b, preferred_element_type=F32)


def dot_t(a, b):
    return lax.dot_general(a, b, (((1,), (1,)), ((), ())), preferred_element_type=F32)


def kernel(
    emb,
    w_own,
    w_out,
    w_gate,
    norm_gain,
    head_gain,
    bias,
    owner,
    out,
    out_mem,
    out_aux,
    xb,
    wb,
    wo,
    qs,
    ks,
    vs,
    gs,
    num,
    den,
    rows_in,
    cols_in,
    sum_c,
    sum_aux,
    pair_c,
    pair_aux,
    state_c,
    hn,
    act,
    own_p,
    total,
    rows_got,
    mem_got,
    aux_got,
    aux_out,
    send_sem,
    local_sem,
    sem_a,
    sem_ring,
    sem_sib,
    sem_w,
    sem_wz,
    sem_wo,
    sem_woz,
    sem_wos,
    sem_mate,
    sem_pair,
    sem_hn,
    sem_act,
    sem_out,
    sem_mem,
):
    c = lax.axis_index("ctx")
    h = lax.axis_index("hr")
    x, y = h // 4, h % 4
    z, k = c // 2, c % 2
    req, par = y // 2, y % 2

    def dev(x_, y_, z_, k_):
        return (z_ * 2 + k_, x_ * 4 + y_)

    def rel(base, step):
        return lax.rem(base + step, 4)

    sib = dev(x, y, z, 1 - k)
    x_next, x_prev = dev(rel(x, 1), y, z, k), dev(rel(x, 3), y, z, k)
    y_next, y_prev = dev(x, rel(y, 1), z, k), dev(x, rel(y, 3), z, k)
    z_next, z_prev = dev(x, y, rel(z, 1), k), dev(x, y, rel(z, 3), k)
    mate = dev(x, 2 * req + 1 - par, z, k)

    partners = [sib]
    for step in (1, 2, 3):
        for core in (0, 1):
            partners.append(dev(x, rel(y, step), z, core))
        partners.append(dev(rel(x, step), y, z, k))
        partners.append(dev(x, y, rel(z, step), k))
    barrier = pltpu.get_barrier_semaphore()
    for partner in partners:
        pl.semaphore_signal(barrier, inc=1, device_id=partner, device_id_type=MESH)
    pl.semaphore_wait(barrier, len(partners))

    pending = []

    def push(src, dst, sem, target, when=None):
        slot = len(pending)
        copy = pltpu.make_async_remote_copy(
            src_ref=src,
            dst_ref=dst,
            send_sem=send_sem.at[slot],
            recv_sem=sem,
            device_id=target,
            device_id_type=MESH,
        )
        pending.append((copy, when))
        if when is None:
            copy.start()
        else:
            pl.when(when)(copy.start)

    def here(src, dst, sem, when):
        copy = pltpu.make_async_copy(src, dst, sem)
        pl.when(when)(copy.start)

    def arrived(dst, sem, when=None):
        copy = pltpu.make_async_remote_copy(
            src_ref=dst,
            dst_ref=dst,
            send_sem=send_sem.at[0],
            recv_sem=sem,
            device_id=sib,
            device_id_type=MESH,
        )
        if when is None:
            copy.wait_recv()
        else:
            pl.when(when)(copy.wait_recv)

    k_half = k * HALF
    xl, xr, xo = rel(x, 3), rel(x, 1), rel(x, 2)
    zl, zr, zo = rel(z, 3), rel(z, 1), rel(z, 2)

    for piece in range(PIECES):
        for r_ in (0, 1):
            for kd in (0, 1):
                y_to = 2 * r_ + k
                mine = (y_to == y) & (kd == k)
                start = kd * HALF + piece * PIECE
                src = emb.at[r_, pl.ds(start, PIECE), :]
                dst = xb.at[x, pl.ds(start, PIECE), pl.ds(pl.multiple_of(y * 256, 256), 256)]
                push(src, dst, sem_a.at[piece, y], dev(x, y_to, z, kd), jnp.logical_not(mine))
                here(src, dst, sem_a.at[piece, y], mine)

    w_local = pltpu.make_async_copy(w_own, wb.at[y % 2], local_sem.at[0])
    pl.when(k == y // 2)(w_local.start)
    o_local = pltpu.make_async_copy(w_out, wo.at[y], local_sem.at[1])
    o_local.start()

    def rows_of(block, core, piece, half=None):
        start, size = core * HALF + piece * PIECE, PIECE
        if half is not None:
            start, size = start + half * (PIECE // 2), PIECE // 2
        return xb.at[block, pl.ds(start, size), :]

    def ring_start(piece):
        for y_ in range(4):
            arrived(
                xb.at[x, pl.ds(k_half + piece * PIECE, PIECE), pl.ds(y_ * 256, 256)],
                sem_a.at[piece, y_],
            )
        block = rows_of(x, k, piece)
        push(block, block, sem_ring.at[0, piece], x_next)
        push(block, block, sem_ring.at[1, piece], x_prev)
        push(block, block, sem_sib.at[0, piece], sib)

    def ring_middle(piece):
        block = rows_of(xl, k, piece)
        arrived(block, sem_ring.at[0, piece])
        half = rows_of(xl, k, piece, 0)
        push(half, half, sem_ring.at[2, piece], x_next)
        push(block, block, sem_sib.at[1, piece], sib)
        block = rows_of(xr, k, piece)
        arrived(block, sem_ring.at[1, piece])
        half = rows_of(xr, k, piece, 1)
        push(half, half, sem_ring.at[3, piece], x_prev)
        push(block, block, sem_sib.at[2, piece], sib)

    def ring_end(piece):
        for half in (0, 1):
            arrived(rows_of(xo, k, piece, half), sem_ring.at[2 + half, piece])
        block = rows_of(xo, k, piece)
        push(block, block, sem_sib.at[3, piece], sib)

    def w_part(kind, j, plane, part, half=None):
        if kind == 0:
            start, size = (plane * 2 + part) * SPREAD, SPREAD
        else:
            start, size = 8 * SPREAD + part * DIRECT, DIRECT
        if half is not None:
            start, size = start + half * (size // 2), size // 2
        if not isinstance(start, int):
            start = pl.multiple_of(start, 32)
        return (j, pl.ds(start, size), slice(None))

    def w_send(kind):
        at = w_part(kind, y % 2, z, k)
        src = w_own.at[at[1], at[2]]
        core = y // 2
        push(src, wb.at[at], sem_w.at[kind, y % 2, k, 0], dev(x, rel(y, 1), z, core))
        push(src, wb.at[at], sem_w.at[kind, y % 2, k, 0], dev(x, rel(y, 3), z, core))

    away = [lax.rem(y - 2 * k - j + 4, 4) for j in (0, 1)]
    foreign = [step != 0 for step in away]

    def w_near(kind):
        for j in (0, 1):
            near = (away[j] == 1) | (away[j] == 3)
            for part in (0, 1):
                arrived(wb.at[w_part(kind, j, z, part)], sem_w.at[kind, j, part, 0], near)
                half = wb.at[w_part(kind, j, z, part, 0)]
                push(half, half, sem_w.at[kind, j, part, 0], y_next, away[j] == 1)
                half = wb.at[w_part(kind, j, z, part, 1)]
                push(half, half, sem_w.at[kind, j, part, 1], y_prev, away[j] == 3)

    def w_far(kind):
        for j in (0, 1):
            for part in (0, 1):
                for half in (0, 1):
                    arrived(
                        wb.at[w_part(kind, j, z, part, half)],
                        sem_w.at[kind, j, part, half],
                        away[j] == 2,
                    )

    def w_along_z(distances):
        for j in (0, 1):
            right = away[j] == distances[0]
            for other in distances[1:]:
                right = right | (away[j] == other)
            for part in (0, 1):
                block = wb.at[w_part(0, j, z, part)]
                push(block, block, sem_wz.at[0, j, part], z_next, right)
                push(block, block, sem_wz.at[1, j, part], z_prev, right)

    ring_start(0)
    w_send(0)
    ring_start(1)
    w_near(0)
    w_along_z((1, 3))
    w_send(1)
    ring_middle(0)
    w_far(0)
    w_along_z((2,))
    ring_middle(1)
    w_near(1)

    def o_part(y_, plane, core, half=None):
        start, size = plane * 1024 + core * 512, 512
        if half is not None:
            start, size = start + half * 256, 256
        return wo.at[y_, pl.ds(pl.multiple_of(start, 256), size), :]

    for step in (1, 3, 2):
        push(
            w_out.at[pl.ds(pl.multiple_of(z * 1024 + k * 512, 512), 512), :],
            o_part(y, z, k),
            sem_wo.at[y],
            dev(x, rel(y, step), z, k),
        )

    for j in (0, 1):
        for part in (0, 1):
            from_left, from_right = wb.at[w_part(0, j, zl, part)], wb.at[w_part(0, j, zr, part)]
            arrived(from_left, sem_wz.at[0, j, part], foreign[j])
            arrived(from_right, sem_wz.at[1, j, part], foreign[j])
            if part == 0:
                push(from_left, from_left, sem_wz.at[2, j, 0], z_next, foreign[j])
            else:
                push(from_right, from_right, sem_wz.at[2, j, 1], z_prev, foreign[j])

    ring_end(0)
    ring_end(1)
    w_far(1)
    pl.when(k == y // 2)(w_local.wait)
    for j in (0, 1):
        for part in (0, 1):
            arrived(wb.at[w_part(0, j, zo, part)], sem_wz.at[2, j, part], foreign[j])

    others = [rel(y, step) for step in (1, 2, 3)]
    for index, y_ in enumerate(others):
        block = o_part(y_, z, k)
        arrived(block, sem_wo.at[y_])
        push(block, block, sem_woz.at[0, index], z_next)
        push(block, block, sem_woz.at[1, index], z_prev)
        push(block, block, sem_wos.at[0, index], sib)

    for index, block_x in enumerate((x, xl, xr, xo)):
        for piece in range(PIECES):
            arrived(rows_of(block_x, 1 - k, piece), sem_sib.at[index, piece])

    def project(step, carry):
        rows = pl.ds(pl.multiple_of(step * TILE, TILE), TILE)
        squares = jnp.zeros((TILE, 1), F32)
        for block in range(4):
            wide = xb[block, rows, :].astype(F32)
            squares += jnp.sum(wide * wide, axis=1, keepdims=True)
        scale = lax.rsqrt(squares / WIDTH + epsilon)
        accs = [jnp.zeros((TILE, 512), F32), jnp.zeros((TILE, 512), F32)]
        gate = jnp.zeros((16, TILE), F32)
        for block in range(4):
            depth = slice(block * 1024, block * 1024 + 1024)
            wide = xb[block, rows, :].astype(F32)
            normed = (wide * scale * norm_gain[block : block + 1, :]).astype(BF16)
            for j in (0, 1):
                accs[j] = accs[j] + dot(normed, wb[j, depth, :])
            gate = gate + dot_t(w_gate[:, depth], normed)
        qs[rows, :] = accs[0][:, :KEY].astype(BF16)
        ks[rows, :] = accs[0][:, KEY:].astype(BF16)
        vs[rows, :] = accs[1].astype(BF16)
        gs[:, rows] = gate
        return carry

    lax.fori_loop(0, ROWS // TILE, project, 0)

    head = 2 * x + k
    gates = gs[...]
    sub = lax.broadcasted_iota(jnp.int32, (16, ROWS), 0)
    gate_in = jnp.sum(jnp.where(sub == head, gates, 0.0), axis=0, keepdims=True)
    pre_forget = jnp.sum(jnp.where(sub == head + 8, gates, 0.0), axis=0, keepdims=True)
    gate_in = jnp.broadcast_to(gate_in, (8, ROWS)) + bias[0, head]
    pre_forget = jnp.broadcast_to(pre_forget, (8, ROWS)) + bias[1, head]
    log_forget = jnp.minimum(pre_forget, 0.0) - jnp.log1p(jnp.exp(-jnp.abs(pre_forget)))
    lane = lax.broadcasted_iota(jnp.int32, (8, ROWS), 1)
    cum = log_forget
    step = 1
    while step < ROWS:
        cum = cum + jnp.where(lane >= step, pltpu.roll(cum, step, 1), 0.0)
        step *= 2
    lead = gate_in - cum
    peak = lead
    step = 1
    while step < ROWS:
        peak = jnp.maximum(peak, jnp.where(lane >= step, pltpu.roll(peak, step, 1), very_negative))
        step *= 2
    rows_in[0:8, :] = cum
    rows_in[8:16, :] = lead
    rows_in[16:24, :] = peak
    last_peak = jnp.max(lead, axis=1, keepdims=True)[0:1, :]
    decay = jnp.sum(jnp.where(lane == ROWS - 1, cum, 0.0), axis=1, keepdims=True)[0:1, :]
    rows_in[24:32, :] = jnp.exp(lead - last_peak)
    rows_in[32:, :] = jnp.zeros((96, ROWS), F32)
    cols_in[...] = rows_in[...].T

    scaled = ks[...].astype(F32) * cols_in[:, 24:25]
    norm_sum = jnp.sum(scaled, axis=0, keepdims=True)
    memory = lax.dot_general(
        scaled.astype(BF16), vs[...], (((0,), (0,)), ((), ())), preferred_element_type=F32
    )
    sum_c[par] = memory.astype(BF16)
    row = lax.broadcasted_iota(jnp.int32, (8, KEY), 0)
    sum_aux[par] = jnp.where(row == 0, norm_sum, jnp.where(row == 1, decay + last_peak, decay))
    push(sum_aux.at[par], sum_aux.at[par], sem_mate.at[0], mate)
    push(sum_c.at[par], sum_c.at[par], sem_mate.at[1], mate)

    lead_row = rows_in[8:9, :]

    def within(index):
        rows = slice(index * TILE, (index + 1) * TILE)
        seen = (index + 1) * TILE
        scores = dot_t(qs[rows, :], ks[:seen, :])
        t_at = lax.broadcasted_iota(jnp.int32, (TILE, seen), 0) + index * TILE
        s_at = lax.broadcasted_iota(jnp.int32, (TILE, seen), 1)
        exponent = jnp.where(t_at >= s_at, lead_row[:, :seen] - cols_in[rows, 16:17], very_negative)
        weighted = jnp.exp(exponent) * (scores * 0.0625)
        num[rows, :] = dot(weighted.astype(BF16), vs[:seen, :])
        den[rows, :] = jnp.broadcast_to(jnp.sum(weighted, axis=1, keepdims=True), (TILE, 128))

    def twice(value):
        return jnp.concatenate([value, value], axis=1)

    def join(state, c_ref, aux_ref, at):
        decay_, top, norm = state
        later = aux_ref[at]
        peak_, falls = later[1:2, :], later[2:3, :]
        joined = jnp.maximum(falls + top, peak_)
        one, two = jnp.exp(falls + top - joined), jnp.exp(peak_ - joined)
        state_c[...] = twice(one) * state_c[...] + twice(two) * c_ref[at].astype(F32)
        return decay_ + falls, joined, one * norm + two * later[0:1, :]

    def start_state():
        state_c[...] = jnp.zeros_like(state_c)
        zero = jnp.zeros((1, KEY), F32)
        return zero, jnp.full((1, KEY), very_negative, F32), zero

    for index in (0, 1):
        within(index)
    other = 1 - par
    arrived(sum_aux.at[other], sem_mate.at[0])
    arrived(sum_c.at[other], sem_mate.at[1])
    state = start_state()
    for at in (0, 1):
        state = join(state, sum_c, sum_aux, at)
    pair_c[z] = state_c[...].astype(BF16)
    pair_aux[z] = jnp.where(row == 0, state[2], jnp.where(row == 1, state[1], state[0]))
    for step in (1, 3, 2):
        to = dev(x, y, rel(z, step), k)
        push(pair_aux.at[z], pair_aux.at[z], sem_pair.at[0, z], to)
        push(pair_c.at[z], pair_c.at[z], sem_pair.at[1, z], to)
    for index in (2, 3):
        within(index)

    for step in (1, 3, 2):
        z_ = rel(z, step)
        arrived(pair_aux.at[z_], sem_pair.at[0, z_])
        arrived(pair_c.at[z_], sem_pair.at[1, z_])

    for index, y_ in enumerate(others):
        from_left, from_right = o_part(y_, zl, k), o_part(y_, zr, k)
        arrived(from_left, sem_woz.at[0, index])
        arrived(from_right, sem_woz.at[1, index])
        half = o_part(y_, zl, k, 0)
        push(half, half, sem_woz.at[2, index], z_next)
        half = o_part(y_, zr, k, 1)
        push(half, half, sem_woz.at[3, index], z_prev)

    def pairs(limit):
        return lax.fori_loop(
            0, limit, lambda at, state: join(state, pair_c, pair_aux, at), start_state()
        )

    state = pairs(z)
    _, top_in, norm_in = lax.fori_loop(
        0, par, lambda at, state: join(state, sum_c, sum_aux, at), state
    )
    sub8 = lax.broadcasted_iota(jnp.int32, (8, VAL), 0)
    gain = jnp.sum(
        jnp.where(sub8 == head, head_gain[...].astype(F32), 0.0), axis=0, keepdims=True
    )
    memory_in = state_c[...].astype(BF16)

    def finish(start):
        rows = pl.ds(pl.multiple_of(start, TILE), TILE)
        q = qs[rows, :]
        carried = dot(q, memory_in) * 0.0625
        carried_norm = jnp.sum(q.astype(F32) * norm_in, axis=1, keepdims=True) * 0.0625
        columns = cols_in[rows, :]
        here_max = columns[:, 16:17]
        both = jnp.maximum(top_in[:, 0:1], here_max)
        inner, outer = jnp.exp(here_max - both), jnp.exp(top_in[:, 0:1] - both)
        row_max = columns[:, 0:1] + both
        bottom = inner * den[rows, :][:, 0:1] + outer * carried_norm
        divisor = jnp.maximum(jnp.abs(bottom), jnp.exp(-row_max))
        hidden = (inner * num[rows, :] + outer * carried) / divisor
        scale = lax.rsqrt(jnp.mean(hidden * hidden, axis=1, keepdims=True) + epsilon)
        return (hidden * scale * gain).astype(BF16)

    def act_of(block, kk, tile, half=None):
        start, size = tile * TILE, TILE
        if half is not None:
            start, size = start + half * (TILE // 2), TILE // 2
        return act.at[block, kk, pl.ds(start, size), :]

    def act_start(kk, order, tile):
        block = act_of(x, kk, tile)
        push(block, block, sem_act.at[0, order, tile], x_next)
        push(block, block, sem_act.at[1, order, tile], x_prev)

    for tile in (0, 1):
        act[x, k, tile * TILE : (tile + 1) * TILE, :] = finish(k_half + tile * TILE)
        act_start(k, 0, tile)
    for tile in (0, 1):
        rows = slice(tile * TILE, (tile + 1) * TILE)
        hn[rows, :] = finish((1 - k) * HALF + tile * TILE)
        push(hn.at[rows, :], act_of(x, k, tile), sem_hn.at[tile], sib)
    for tile in (0, 1):
        arrived(act_of(x, 1 - k, tile), sem_hn.at[tile])
        act_start(1 - k, 1, tile)

    for index, y_ in enumerate(others):
        block = o_part(y_, zl, k)
        push(block, block, sem_wos.at[1, index], sib)
        block = o_part(y_, zr, k)
        push(block, block, sem_wos.at[2, index], sib)
        arrived(o_part(y_, zo, k, 0), sem_woz.at[2, index])
        arrived(o_part(y_, zo, k, 1), sem_woz.at[3, index])
        block = o_part(y_, zo, k)
        push(block, block, sem_wos.at[3, index], sib)

    for order, kk in ((0, k), (1, 1 - k)):
        for tile in (0, 1):
            arrived(act_of(xl, kk, tile), sem_act.at[0, order, tile])
            half = act_of(xl, kk, tile, 0)
            push(half, half, sem_act.at[2, order, tile], x_next)
            arrived(act_of(xr, kk, tile), sem_act.at[1, order, tile])
            half = act_of(xr, kk, tile, 1)
            push(half, half, sem_act.at[3, order, tile], x_prev)

    _, top_end, norm_end = pairs(4)
    aux_out[...] = jnp.where(row == 0, norm_end, top_end)
    keep_here = (k == req) & (par == k)
    mem_to = dev(x, 2 * k + req, z, par)
    push(state_c, mem_got, sem_mem.at[0], mem_to, jnp.logical_not(keep_here))
    push(aux_out, aux_got, sem_mem.at[1], mem_to, jnp.logical_not(keep_here))
    here(state_c, mem_got, sem_mem.at[0], keep_here)
    here(aux_out, aux_got, sem_mem.at[1], keep_here)

    o_local.wait()
    for index, y_ in enumerate(others):
        for at, plane in enumerate((z, zl, zr, zo)):
            arrived(o_part(y_, plane, 1 - k), sem_wos.at[at, index])

    def mixed(block, tile, y_):
        rows = slice(tile * TILE, (tile + 1) * TILE)
        start = pl.multiple_of(block * 1024, 1024)
        return dot(act[block, 0, rows, :], wo[y_, pl.ds(start, 512), :]) + dot(
            act[block, 1, rows, :], wo[y_, pl.ds(start + 512, 512), :]
        )

    for tile in (0, 1):
        for y_ in range(4):
            own_p[tile * TILE : (tile + 1) * TILE, y_ * 256 : y_ * 256 + 256] = (
                mixed(x, tile, y_) + mixed(xl, tile, y_) + mixed(xr, tile, y_)
            )
    for tile in (0, 1):
        rows = slice(tile * TILE, (tile + 1) * TILE)
        for order, kk in ((0, k), (1, 1 - k)):
            for half in (0, 1):
                arrived(act_of(xo, kk, tile, half), sem_act.at[2 + half, order, tile])
        for y_ in range(4):
            cols = slice(y_ * 256, y_ * 256 + 256)
            total[rows, cols] = (own_p[rows, cols] + mixed(xo, tile, y_)).astype(BF16)
            src = total.at[rows, cols]
            dst = rows_got.at[req, pl.ds(pl.multiple_of(k_half + tile * TILE, TILE), TILE), :]
            mine = (y == y_) & (par == k)
            push(src, dst, sem_out.at[tile, req, k], dev(x, y_, z, par), jnp.logical_not(mine))
            here(src, dst, sem_out.at[tile, req, k], mine)

    arrived(mem_got, sem_mem.at[0])
    arrived(aux_got, sem_mem.at[1])
    keep = jnp.where(owner[h] == c, 1.0, 0.0)
    out_mem[...] = mem_got[...] * keep
    out_aux[...] = aux_got[...] * keep
    for tile in (0, 1):
        for r_ in (0, 1):
            for k_ in (0, 1):
                rows = slice(k_ * HALF + tile * TILE, k_ * HALF + (tile + 1) * TILE)
                arrived(rows_got.at[r_, rows, :], sem_out.at[tile, r_, k_])
                out[r_, rows, :] = (
                    emb[r_, rows, :].astype(F32) + rows_got[r_, rows, :].astype(F32)
                ).astype(BF16)
    for copy, when in pending:
        if when is None:
            copy.wait_send()
        else:
            pl.when(when)(copy.wait_send)


def local(token_ids, embed_table, norm_gain, w_qkv, w_gate, gate_bias, head_gain, w_out, owner):
    embedded = embed_table.at[token_ids].get(mode="promise_in_bounds")
    gates = jnp.transpose(w_gate, (1, 2, 0)).reshape(16, WIDTH)
    vmem = pl.BlockSpec(memory_space=pltpu.VMEM)
    smem = pl.BlockSpec(memory_space=pltpu.SMEM)
    hbm = pl.BlockSpec(memory_space=pl.ANY)
    dma = pltpu.SemaphoreType.DMA
    block_out, mem, aux = pl.pallas_call(
        kernel,
        out_shape=(
            jax.ShapeDtypeStruct((2, ROWS, 256), BF16),
            jax.ShapeDtypeStruct((KEY, VAL), F32),
            jax.ShapeDtypeStruct((8, KEY), F32),
        ),
        in_specs=[vmem, hbm, hbm, vmem, vmem, vmem, smem, smem],
        out_specs=(vmem, vmem, vmem),
        scratch_shapes=[
            pltpu.VMEM((4, ROWS, 1024), BF16),
            pltpu.VMEM((2, WIDTH, 512), BF16),
            pltpu.VMEM((4, WIDTH, 256), BF16),
            pltpu.VMEM((ROWS, KEY), BF16),
            pltpu.VMEM((ROWS, KEY), BF16),
            pltpu.VMEM((ROWS, VAL), BF16),
            pltpu.VMEM((16, ROWS), F32),
            pltpu.VMEM((ROWS, VAL), F32),
            pltpu.VMEM((ROWS, 128), F32),
            pltpu.VMEM((128, ROWS), F32),
            pltpu.VMEM((ROWS, 128), F32),
            pltpu.VMEM((2, KEY, VAL), BF16),
            pltpu.VMEM((2, 8, KEY), F32),
            pltpu.VMEM((4, KEY, VAL), BF16),
            pltpu.VMEM((4, 8, KEY), F32),
            pltpu.VMEM((KEY, VAL), F32),
            pltpu.VMEM((HALF, VAL), BF16),
            pltpu.VMEM((4, 2, HALF, VAL), BF16),
            pltpu.VMEM((HALF, 1024), F32),
            pltpu.VMEM((HALF, 1024), BF16),
            pltpu.VMEM((2, ROWS, 256), BF16),
            pltpu.VMEM((KEY, VAL), F32),
            pltpu.VMEM((8, KEY), F32),
            pltpu.VMEM((8, KEY), F32),
            dma((SENDS,)),
            dma((2,)),
            dma((PIECES, 4)),
            dma((4, PIECES)),
            dma((4, PIECES)),
            dma((2, 2, 2, 2)),
            dma((3, 2, 2)),
            dma((4,)),
            dma((4, 3)),
            dma((4, 3)),
            dma((2,)),
            dma((2, 4)),
            dma((2,)),
            dma((4, 2, 2)),
            dma((2, 2, 2)),
            dma((2,)),
        ],
        compiler_params=pltpu.CompilerParams(
            collective_id=0, has_side_effects=True, vmem_limit_bytes=60 * 2**20
        ),
    )(
        embedded,
        w_qkv.reshape(WIDTH, 512),
        w_out,
        gates,
        norm_gain.astype(F32).reshape(4, 1024),
        head_gain,
        gate_bias,
        owner,
    )
    memory_c = mem[None, None, None]
    memory_n = aux[0][None, None, None]
    memory_m = aux[1, 0:1][None, None]
    return (block_out, memory_c, memory_n, memory_m)


def solution(mesh):
    return jax.shard_map(
        local,
        mesh=mesh,
        in_specs=(
            P(None, "ctx"),
            P(None, "hr"),
            P(),
            P(None, "hr", None, None),
            P(),
            P(),
            P(),
            P(None, "hr"),
            P(),
        ),
        out_specs=(
            P(None, "ctx", "hr"),
            P("ctx", "hr", None, None, None),
            P("ctx", "hr", None, None),
            P("ctx", "hr", None),
        ),
        check_vma=False,
    )
```

```python
import jax
import jax.numpy as jnp
from jax import lax
from jax.experimental import pallas as pl
from jax.experimental.pallas import tpu as pltpu
from jax.sharding import PartitionSpec as P

MESH = pl.DeviceIdType.MESH
F32 = jnp.float32
BF16 = jnp.bfloat16
very_negative = -1e30
epsilon = 1e-06

WIDTH = 4096
ROWS = 1024
HALF = 512
PIECES = 2
PIECE = HALF // PIECES
KEY = 256
VAL = 512
SENDS = 128
SPREAD = 384
DIRECT = 512
TILE = 256


def dot(a, b):
    return jnp.dot(a, b, preferred_element_type=F32)


def dot_t(a, b):
    return lax.dot_general(a, b, (((1,), (1,)), ((), ())), preferred_element_type=F32)


def kernel(
    ids,
    table,
    w_own,
    w_out,
    w_gate,
    norm_gain,
    head_gain,
    bias,
    owner,
    out,
    out_mem,
    out_aux,
    tbl,
    emb,
    xb,
    wb,
    wo,
    qs,
    ks,
    vs,
    gs,
    scales,
    num,
    den,
    rows_in,
    cols_in,
    sum_c,
    sum_aux,
    pair_c,
    pair_aux,
    state_c,
    hn,
    act,
    own_p,
    total,
    rows_got,
    mem_got,
    aux_got,
    aux_out,
    send_sem,
    local_sem,
    sem_tbl,
    sem_a,
    sem_ring,
    sem_sib,
    sem_w,
    sem_wz,
    sem_wo,
    sem_woz,
    sem_wos,
    sem_mate,
    sem_pair,
    sem_hn,
    sem_act,
    sem_out,
    sem_mem,
):
    c = lax.axis_index("ctx")
    h = lax.axis_index("hr")
    x, y = h // 4, h % 4
    z, k = c // 2, c % 2
    req, par = y // 2, y % 2

    def dev(x_, y_, z_, k_):
        return (z_ * 2 + k_, x_ * 4 + y_)

    def rel(base, step):
        return lax.rem(base + step, 4)

    sib = dev(x, y, z, 1 - k)
    x_next, x_prev = dev(rel(x, 1), y, z, k), dev(rel(x, 3), y, z, k)
    y_next, y_prev = dev(x, rel(y, 1), z, k), dev(x, rel(y, 3), z, k)
    z_next, z_prev = dev(x, y, rel(z, 1), k), dev(x, y, rel(z, 3), k)
    mate = dev(x, 2 * req + 1 - par, z, k)

    copies = []
    for part in range(4):
        rows = pl.ds(part * 1024, 1024)
        copies.append(pltpu.make_async_copy(table.at[rows], tbl.at[rows], sem_tbl.at[part]))
        copies[-1].start()

    partners = [sib]
    for step in (1, 2, 3):
        for core in (0, 1):
            partners.append(dev(x, rel(y, step), z, core))
        partners.append(dev(rel(x, step), y, z, k))
        partners.append(dev(x, y, rel(z, step), k))
    barrier = pltpu.get_barrier_semaphore()
    for partner in partners:
        pl.semaphore_signal(barrier, inc=1, device_id=partner, device_id_type=MESH)
    pl.semaphore_wait(barrier, len(partners))

    pending = []

    def push(src, dst, sem, target, when=None):
        slot = len(pending)
        copy = pltpu.make_async_remote_copy(
            src_ref=src,
            dst_ref=dst,
            send_sem=send_sem.at[slot],
            recv_sem=sem,
            device_id=target,
            device_id_type=MESH,
        )
        pending.append((copy, when))
        if when is None:
            copy.start()
        else:
            pl.when(when)(copy.start)

    def here(src, dst, sem, when):
        copy = pltpu.make_async_copy(src, dst, sem)
        pl.when(when)(copy.start)

    def arrived(dst, sem, when=None):
        copy = pltpu.make_async_remote_copy(
            src_ref=dst,
            dst_ref=dst,
            send_sem=send_sem.at[0],
            recv_sem=sem,
            device_id=sib,
            device_id_type=MESH,
        )
        if when is None:
            copy.wait_recv()
        else:
            pl.when(when)(copy.wait_recv)

    k_half = k * HALF
    xl, xr, xo = rel(x, 3), rel(x, 1), rel(x, 2)
    zl, zr, zo = rel(z, 3), rel(z, 1), rel(z, 2)

    sub_tile = lax.broadcasted_iota(jnp.int32, (8, 256), 0)

    def look(r_, start):
        def body(step, carry):
            base = pl.multiple_of(start + step * 16, 16)
            eights = []
            for eight in (0, 1):
                found = jnp.zeros((8, 256), F32)
                for t in range(8):
                    token = ids[r_, base + eight * 8 + t]
                    turned = pltpu.roll(
                        tbl[lax.shift_right_logical(token, 3)].astype(F32),
                        lax.rem(t + 8 - lax.rem(token, 8), 8),
                        0,
                    )
                    found = jnp.where(sub_tile == t, turned, found)
                eights.append(found)
            emb[r_, pl.ds(base, 16), :] = jnp.concatenate(eights, axis=0).astype(BF16)
            return carry

        lax.fori_loop(0, PIECE // 16, body, 0)

    def look_and_send(piece):
        for r_ in (0, 1):
            for kd in (0, 1):
                y_to = 2 * r_ + k
                mine = (y_to == y) & (kd == k)
                start = kd * HALF + piece * PIECE
                look(r_, start)
                src = emb.at[r_, pl.ds(start, PIECE), :]
                dst = xb.at[x, pl.ds(start, PIECE), pl.ds(pl.multiple_of(y * 256, 256), 256)]
                push(src, dst, sem_a.at[piece, y], dev(x, y_to, z, kd), jnp.logical_not(mine))
                here(src, dst, sem_a.at[piece, y], mine)

    w_local = pltpu.make_async_copy(w_own, wb.at[y % 2], local_sem.at[0])
    o_local = pltpu.make_async_copy(w_out, wo.at[y], local_sem.at[1])

    def rows_of(block, core, piece, half=None):
        start, size = core * HALF + piece * PIECE, PIECE
        if half is not None:
            start, size = start + half * (PIECE // 2), PIECE // 2
        return xb.at[block, pl.ds(start, size), :]

    def ring_start(piece):
        for y_ in range(4):
            arrived(
                xb.at[x, pl.ds(k_half + piece * PIECE, PIECE), pl.ds(y_ * 256, 256)],
                sem_a.at[piece, y_],
            )
        block = rows_of(x, k, piece)
        push(block, block, sem_ring.at[0, piece], x_next)
        push(block, block, sem_ring.at[1, piece], x_prev)
        push(block, block, sem_sib.at[0, piece], sib)

    def ring_middle(piece):
        block = rows_of(xl, k, piece)
        arrived(block, sem_ring.at[0, piece])
        half = rows_of(xl, k, piece, 0)
        push(half, half, sem_ring.at[2, piece], x_next)
        push(block, block, sem_sib.at[1, piece], sib)
        block = rows_of(xr, k, piece)
        arrived(block, sem_ring.at[1, piece])
        half = rows_of(xr, k, piece, 1)
        push(half, half, sem_ring.at[3, piece], x_prev)
        push(block, block, sem_sib.at[2, piece], sib)

    def ring_end(piece):
        for half in (0, 1):
            arrived(rows_of(xo, k, piece, half), sem_ring.at[2 + half, piece])
        block = rows_of(xo, k, piece)
        push(block, block, sem_sib.at[3, piece], sib)

    def w_part(kind, j, plane, part, half=None):
        if kind == 0:
            start, size = (plane * 2 + part) * SPREAD, SPREAD
        else:
            start, size = 8 * SPREAD + part * DIRECT, DIRECT
        if half is not None:
            start, size = start + half * (size // 2), size // 2
        if not isinstance(start, int):
            start = pl.multiple_of(start, 32)
        return (j, pl.ds(start, size), slice(None))

    def w_send(kind):
        at = w_part(kind, y % 2, z, k)
        src = w_own.at[at[1], at[2]]
        core = y // 2
        push(src, wb.at[at], sem_w.at[kind, y % 2, k, 0], dev(x, rel(y, 1), z, core))
        push(src, wb.at[at], sem_w.at[kind, y % 2, k, 0], dev(x, rel(y, 3), z, core))

    away = [lax.rem(y - 2 * k - j + 4, 4) for j in (0, 1)]
    foreign = [step != 0 for step in away]

    def w_near(kind):
        for j in (0, 1):
            near = (away[j] == 1) | (away[j] == 3)
            for part in (0, 1):
                arrived(wb.at[w_part(kind, j, z, part)], sem_w.at[kind, j, part, 0], near)
                half = wb.at[w_part(kind, j, z, part, 0)]
                push(half, half, sem_w.at[kind, j, part, 0], y_next, away[j] == 1)
                half = wb.at[w_part(kind, j, z, part, 1)]
                push(half, half, sem_w.at[kind, j, part, 1], y_prev, away[j] == 3)

    def w_far(kind):
        for j in (0, 1):
            for part in (0, 1):
                for half in (0, 1):
                    arrived(
                        wb.at[w_part(kind, j, z, part, half)],
                        sem_w.at[kind, j, part, half],
                        away[j] == 2,
                    )

    def w_along_z(distances):
        for j in (0, 1):
            right = away[j] == distances[0]
            for other in distances[1:]:
                right = right | (away[j] == other)
            for part in (0, 1):
                block = wb.at[w_part(0, j, z, part)]
                push(block, block, sem_wz.at[0, j, part], z_next, right)
                push(block, block, sem_wz.at[1, j, part], z_prev, right)

    w_send(0)
    for copy in copies:
        copy.wait()
    pl.when(k == y // 2)(w_local.start)
    o_local.start()
    look_and_send(0)
    w_near(0)
    w_along_z((1, 3))
    look_and_send(1)
    ring_start(0)
    w_far(0)
    w_along_z((2,))
    w_send(1)
    ring_start(1)
    ring_middle(0)
    ring_middle(1)
    w_near(1)

    def o_part(y_, plane, core, half=None):
        start, size = plane * 1024 + core * 512, 512
        if half is not None:
            start, size = start + half * 256, 256
        return wo.at[y_, pl.ds(pl.multiple_of(start, 256), size), :]

    for step in (1, 3, 2):
        push(
            w_out.at[pl.ds(pl.multiple_of(z * 1024 + k * 512, 512), 512), :],
            o_part(y, z, k),
            sem_wo.at[y],
            dev(x, rel(y, step), z, k),
        )

    for j in (0, 1):
        for part in (0, 1):
            from_left, from_right = wb.at[w_part(0, j, zl, part)], wb.at[w_part(0, j, zr, part)]
            arrived(from_left, sem_wz.at[0, j, part], foreign[j])
            arrived(from_right, sem_wz.at[1, j, part], foreign[j])
            if part == 0:
                push(from_left, from_left, sem_wz.at[2, j, 0], z_next, foreign[j])
            else:
                push(from_right, from_right, sem_wz.at[2, j, 1], z_prev, foreign[j])

    ring_end(0)
    ring_end(1)
    w_far(1)
    pl.when(k == y // 2)(w_local.wait)
    for j in (0, 1):
        for part in (0, 1):
            arrived(wb.at[w_part(0, j, zo, part)], sem_wz.at[2, j, part], foreign[j])

    others = [rel(y, step) for step in (1, 2, 3)]
    for index, y_ in enumerate(others):
        block = o_part(y_, z, k)
        arrived(block, sem_wo.at[y_])
        push(block, block, sem_woz.at[0, index], z_next)
        push(block, block, sem_woz.at[1, index], z_prev)
        push(block, block, sem_wos.at[0, index], sib)

    for index, block_x in enumerate((x, xl, xr, xo)):
        for piece in range(PIECES):
            arrived(rows_of(block_x, 1 - k, piece), sem_sib.at[index, piece])

    def norm(block, rows, scale):
        wide = xb[block, rows, :].astype(F32)
        return (wide * scale * norm_gain[block : block + 1, :]).astype(BF16)

    def project(step, carry):
        rows = pl.ds(pl.multiple_of(step * TILE, TILE), TILE)
        squares = jnp.zeros((TILE, 1), F32)
        for block in range(4):
            wide = xb[block, rows, :].astype(F32)
            squares += jnp.sum(wide * wide, axis=1, keepdims=True)
        scale = lax.rsqrt(squares / WIDTH + epsilon)
        scales[rows, :] = jnp.broadcast_to(scale, (TILE, 128))
        keys, values = jnp.zeros((TILE, KEY), F32), jnp.zeros((TILE, VAL), F32)
        gate = jnp.zeros((16, TILE), F32)
        for block in range(4):
            depth = slice(block * 1024, block * 1024 + 1024)
            normed = norm(block, rows, scale)
            keys = keys + dot(normed, wb[0, depth, KEY:])
            values = values + dot(normed, wb[1, depth, :])
            gate = gate + dot_t(w_gate[:, depth], normed)
        ks[rows, :] = keys.astype(BF16)
        vs[rows, :] = values.astype(BF16)
        gs[:, rows] = gate
        return carry

    def project_queries(step, carry):
        rows = pl.ds(pl.multiple_of(step * TILE, TILE), TILE)
        scale = scales[rows, :][:, 0:1]
        queries = jnp.zeros((TILE, KEY), F32)
        for block in range(4):
            normed = norm(block, rows, scale)
            queries = queries + dot(normed, wb[0, block * 1024 : block * 1024 + 1024, :KEY])
        qs[rows, :] = queries.astype(BF16)
        return carry

    lax.fori_loop(0, ROWS // TILE, project, 0)

    head = 2 * x + k
    gates = gs[...]
    sub = lax.broadcasted_iota(jnp.int32, (16, ROWS), 0)
    gate_in = jnp.sum(jnp.where(sub == head, gates, 0.0), axis=0, keepdims=True)
    pre_forget = jnp.sum(jnp.where(sub == head + 8, gates, 0.0), axis=0, keepdims=True)
    gate_in = jnp.broadcast_to(gate_in, (8, ROWS)) + bias[0, head]
    pre_forget = jnp.broadcast_to(pre_forget, (8, ROWS)) + bias[1, head]
    log_forget = jnp.minimum(pre_forget, 0.0) - jnp.log1p(jnp.exp(-jnp.abs(pre_forget)))
    lane = lax.broadcasted_iota(jnp.int32, (8, ROWS), 1)
    cum = log_forget
    step = 1
    while step < ROWS:
        cum = cum + jnp.where(lane >= step, pltpu.roll(cum, step, 1), 0.0)
        step *= 2
    lead = gate_in - cum
    peak = lead
    step = 1
    while step < ROWS:
        peak = jnp.maximum(peak, jnp.where(lane >= step, pltpu.roll(peak, step, 1), very_negative))
        step *= 2
    rows_in[0:8, :] = cum
    rows_in[8:16, :] = lead
    rows_in[16:24, :] = peak
    last_peak = jnp.max(lead, axis=1, keepdims=True)[0:1, :]
    decay = jnp.sum(jnp.where(lane == ROWS - 1, cum, 0.0), axis=1, keepdims=True)[0:1, :]
    rows_in[24:32, :] = jnp.exp(lead - last_peak)
    rows_in[32:, :] = jnp.zeros((96, ROWS), F32)
    cols_in[...] = rows_in[...].T

    scaled = ks[...].astype(F32) * cols_in[:, 24:25]
    norm_sum = jnp.sum(scaled, axis=0, keepdims=True)
    memory = lax.dot_general(
        scaled.astype(BF16), vs[...], (((0,), (0,)), ((), ())), preferred_element_type=F32
    )
    sum_c[par] = memory.astype(BF16)
    row = lax.broadcasted_iota(jnp.int32, (8, KEY), 0)
    sum_aux[par] = jnp.where(row == 0, norm_sum, jnp.where(row == 1, decay + last_peak, decay))
    push(sum_aux.at[par], sum_aux.at[par], sem_mate.at[0], mate)
    push(sum_c.at[par], sum_c.at[par], sem_mate.at[1], mate)

    lax.fori_loop(0, ROWS // TILE, project_queries, 0)

    lead_row = rows_in[8:9, :]

    def within(index):
        rows = slice(index * TILE, (index + 1) * TILE)
        seen = (index + 1) * TILE
        scores = dot_t(qs[rows, :], ks[:seen, :])
        t_at = lax.broadcasted_iota(jnp.int32, (TILE, seen), 0) + index * TILE
        s_at = lax.broadcasted_iota(jnp.int32, (TILE, seen), 1)
        exponent = jnp.where(t_at >= s_at, lead_row[:, :seen] - cols_in[rows, 16:17], very_negative)
        weighted = jnp.exp(exponent) * (scores * 0.0625)
        num[rows, :] = dot(weighted.astype(BF16), vs[:seen, :])
        den[rows, :] = jnp.broadcast_to(jnp.sum(weighted, axis=1, keepdims=True), (TILE, 128))

    def twice(value):
        return jnp.concatenate([value, value], axis=1)

    def join(state, c_ref, aux_ref, at):
        decay_, top, norm = state
        later = aux_ref[at]
        peak_, falls = later[1:2, :], later[2:3, :]
        joined = jnp.maximum(falls + top, peak_)
        one, two = jnp.exp(falls + top - joined), jnp.exp(peak_ - joined)
        state_c[...] = twice(one) * state_c[...] + twice(two) * c_ref[at].astype(F32)
        return decay_ + falls, joined, one * norm + two * later[0:1, :]

    def start_state():
        state_c[...] = jnp.zeros_like(state_c)
        zero = jnp.zeros((1, KEY), F32)
        return zero, jnp.full((1, KEY), very_negative, F32), zero

    other = 1 - par
    arrived(sum_aux.at[other], sem_mate.at[0])
    arrived(sum_c.at[other], sem_mate.at[1])
    state = start_state()
    for at in (0, 1):
        state = join(state, sum_c, sum_aux, at)
    pair_c[z] = state_c[...].astype(BF16)
    pair_aux[z] = jnp.where(row == 0, state[2], jnp.where(row == 1, state[1], state[0]))
    for step in (1, 3, 2):
        to = dev(x, y, rel(z, step), k)
        push(pair_aux.at[z], pair_aux.at[z], sem_pair.at[0, z], to)
        push(pair_c.at[z], pair_c.at[z], sem_pair.at[1, z], to)
    for index in range(4):
        within(index)

    for step in (1, 3, 2):
        z_ = rel(z, step)
        arrived(pair_aux.at[z_], sem_pair.at[0, z_])
        arrived(pair_c.at[z_], sem_pair.at[1, z_])

    for index, y_ in enumerate(others):
        from_left, from_right = o_part(y_, zl, k), o_part(y_, zr, k)
        arrived(from_left, sem_woz.at[0, index])
        arrived(from_right, sem_woz.at[1, index])
        half = o_part(y_, zl, k, 0)
        push(half, half, sem_woz.at[2, index], z_next)
        half = o_part(y_, zr, k, 1)
        push(half, half, sem_woz.at[3, index], z_prev)

    def pairs(limit):
        return lax.fori_loop(
            0, limit, lambda at, state: join(state, pair_c, pair_aux, at), start_state()
        )

    state = pairs(z)
    _, top_in, norm_in = lax.fori_loop(
        0, par, lambda at, state: join(state, sum_c, sum_aux, at), state
    )
    sub8 = lax.broadcasted_iota(jnp.int32, (8, VAL), 0)
    gain = jnp.sum(
        jnp.where(sub8 == head, head_gain[...].astype(F32), 0.0), axis=0, keepdims=True
    )
    memory_in = state_c[...].astype(BF16)

    def finish(start):
        rows = pl.ds(pl.multiple_of(start, TILE), TILE)
        q = qs[rows, :]
        carried = dot(q, memory_in) * 0.0625
        carried_norm = jnp.sum(q.astype(F32) * norm_in, axis=1, keepdims=True) * 0.0625
        columns = cols_in[rows, :]
        here_max = columns[:, 16:17]
        both = jnp.maximum(top_in[:, 0:1], here_max)
        inner, outer = jnp.exp(here_max - both), jnp.exp(top_in[:, 0:1] - both)
        row_max = columns[:, 0:1] + both
        bottom = inner * den[rows, :][:, 0:1] + outer * carried_norm
        divisor = jnp.maximum(jnp.abs(bottom), jnp.exp(-row_max))
        hidden = (inner * num[rows, :] + outer * carried) / divisor
        scale = lax.rsqrt(jnp.mean(hidden * hidden, axis=1, keepdims=True) + epsilon)
        return (hidden * scale * gain).astype(BF16)

    def act_of(block, kk, tile, half=None):
        start, size = tile * TILE, TILE
        if half is not None:
            start, size = start + half * (TILE // 2), TILE // 2
        return act.at[block, kk, pl.ds(start, size), :]

    def act_start(kk, order, tile):
        block = act_of(x, kk, tile)
        push(block, block, sem_act.at[0, order, tile], x_next)
        push(block, block, sem_act.at[1, order, tile], x_prev)

    for tile in (0, 1):
        act[x, k, tile * TILE : (tile + 1) * TILE, :] = finish(k_half + tile * TILE)
        act_start(k, 0, tile)
    for tile in (0, 1):
        rows = slice(tile * TILE, (tile + 1) * TILE)
        hn[rows, :] = finish((1 - k) * HALF + tile * TILE)
        push(hn.at[rows, :], act_of(x, k, tile), sem_hn.at[tile], sib)
    for tile in (0, 1):
        arrived(act_of(x, 1 - k, tile), sem_hn.at[tile])
        act_start(1 - k, 1, tile)

    for index, y_ in enumerate(others):
        block = o_part(y_, zl, k)
        push(block, block, sem_wos.at[1, index], sib)
        block = o_part(y_, zr, k)
        push(block, block, sem_wos.at[2, index], sib)
        arrived(o_part(y_, zo, k, 0), sem_woz.at[2, index])
        arrived(o_part(y_, zo, k, 1), sem_woz.at[3, index])
        block = o_part(y_, zo, k)
        push(block, block, sem_wos.at[3, index], sib)

    for order, kk in ((0, k), (1, 1 - k)):
        for tile in (0, 1):
            arrived(act_of(xl, kk, tile), sem_act.at[0, order, tile])
            half = act_of(xl, kk, tile, 0)
            push(half, half, sem_act.at[2, order, tile], x_next)
            arrived(act_of(xr, kk, tile), sem_act.at[1, order, tile])
            half = act_of(xr, kk, tile, 1)
            push(half, half, sem_act.at[3, order, tile], x_prev)

    _, top_end, norm_end = pairs(4)
    aux_out[...] = jnp.where(row == 0, norm_end, top_end)
    keep_here = (k == req) & (par == k)
    mem_to = dev(x, 2 * k + req, z, par)
    push(state_c, mem_got, sem_mem.at[0], mem_to, jnp.logical_not(keep_here))
    push(aux_out, aux_got, sem_mem.at[1], mem_to, jnp.logical_not(keep_here))
    here(state_c, mem_got, sem_mem.at[0], keep_here)
    here(aux_out, aux_got, sem_mem.at[1], keep_here)

    o_local.wait()
    for index, y_ in enumerate(others):
        for at, plane in enumerate((z, zl, zr, zo)):
            arrived(o_part(y_, plane, 1 - k), sem_wos.at[at, index])

    def mixed(block, tile, y_):
        rows = slice(tile * TILE, (tile + 1) * TILE)
        start = pl.multiple_of(block * 1024, 1024)
        return dot(act[block, 0, rows, :], wo[y_, pl.ds(start, 512), :]) + dot(
            act[block, 1, rows, :], wo[y_, pl.ds(start + 512, 512), :]
        )

    for tile in (0, 1):
        for y_ in range(4):
            own_p[tile * TILE : (tile + 1) * TILE, y_ * 256 : y_ * 256 + 256] = (
                mixed(x, tile, y_) + mixed(xl, tile, y_) + mixed(xr, tile, y_)
            )
    for tile in (0, 1):
        rows = slice(tile * TILE, (tile + 1) * TILE)
        for order, kk in ((0, k), (1, 1 - k)):
            for half in (0, 1):
                arrived(act_of(xo, kk, tile, half), sem_act.at[2 + half, order, tile])
        for y_ in range(4):
            cols = slice(y_ * 256, y_ * 256 + 256)
            total[rows, cols] = (own_p[rows, cols] + mixed(xo, tile, y_)).astype(BF16)
            src = total.at[rows, cols]
            dst = rows_got.at[req, pl.ds(pl.multiple_of(k_half + tile * TILE, TILE), TILE), :]
            mine = (y == y_) & (par == k)
            push(src, dst, sem_out.at[tile, req, k], dev(x, y_, z, par), jnp.logical_not(mine))
            here(src, dst, sem_out.at[tile, req, k], mine)

    arrived(mem_got, sem_mem.at[0])
    arrived(aux_got, sem_mem.at[1])
    keep = jnp.where(owner[h] == c, 1.0, 0.0)
    out_mem[...] = mem_got[...] * keep
    out_aux[...] = aux_got[...] * keep
    for tile in (0, 1):
        for r_ in (0, 1):
            for k_ in (0, 1):
                rows = slice(k_ * HALF + tile * TILE, k_ * HALF + (tile + 1) * TILE)
                arrived(rows_got.at[r_, rows, :], sem_out.at[tile, r_, k_])
                out[r_, rows, :] = (
                    emb[r_, rows, :].astype(F32) + rows_got[r_, rows, :].astype(F32)
                ).astype(BF16)
    for copy, when in pending:
        if when is None:
            copy.wait_send()
        else:
            pl.when(when)(copy.wait_send)


def tail(rows, mem, aux, out, out_c, out_n, out_m):
    out[...] = rows[...]
    out_c[...] = mem[...]
    out_n[...] = aux[0:1, :]
    out_m[...] = aux[1:2, 0:1]


def local(token_ids, embed_table, norm_gain, w_qkv, w_gate, gate_bias, head_gain, w_out, owner):
    gates = jnp.transpose(w_gate, (1, 2, 0)).reshape(16, WIDTH)
    vmem = pl.BlockSpec(memory_space=pltpu.VMEM)
    smem = pl.BlockSpec(memory_space=pltpu.SMEM)
    hbm = pl.BlockSpec(memory_space=pl.ANY)
    dma = pltpu.SemaphoreType.DMA
    block_out, mem, aux = pl.pallas_call(
        kernel,
        out_shape=(
            jax.ShapeDtypeStruct((2, ROWS, 256), BF16),
            jax.ShapeDtypeStruct((KEY, VAL), F32),
            jax.ShapeDtypeStruct((8, KEY), F32),
        ),
        in_specs=[smem, hbm, hbm, hbm, vmem, vmem, vmem, smem, smem],
        out_specs=(vmem, vmem, vmem),
        scratch_shapes=[
            pltpu.VMEM((4096, 8, 256), BF16),
            pltpu.VMEM((2, ROWS, 256), BF16),
            pltpu.VMEM((4, ROWS, 1024), BF16),
            pltpu.VMEM((2, WIDTH, 512), BF16),
            pltpu.VMEM((4, WIDTH, 256), BF16),
            pltpu.VMEM((ROWS, KEY), BF16),
            pltpu.VMEM((ROWS, KEY), BF16),
            pltpu.VMEM((ROWS, VAL), BF16),
            pltpu.VMEM((16, ROWS), F32),
            pltpu.VMEM((ROWS, 128), F32),
            pltpu.VMEM((ROWS, VAL), F32),
            pltpu.VMEM((ROWS, 128), F32),
            pltpu.VMEM((128, ROWS), F32),
            pltpu.VMEM((ROWS, 128), F32),
            pltpu.VMEM((2, KEY, VAL), BF16),
            pltpu.VMEM((2, 8, KEY), F32),
            pltpu.VMEM((4, KEY, VAL), BF16),
            pltpu.VMEM((4, 8, KEY), F32),
            pltpu.VMEM((KEY, VAL), F32),
            pltpu.VMEM((HALF, VAL), BF16),
            pltpu.VMEM((4, 2, HALF, VAL), BF16),
            pltpu.VMEM((HALF, 1024), F32),
            pltpu.VMEM((HALF, 1024), BF16),
            pltpu.VMEM((2, ROWS, 256), BF16),
            pltpu.VMEM((KEY, VAL), F32),
            pltpu.VMEM((8, KEY), F32),
            pltpu.VMEM((8, KEY), F32),
            dma((SENDS,)),
            dma((2,)),
            dma((4,)),
            dma((PIECES, 4)),
            dma((4, PIECES)),
            dma((4, PIECES)),
            dma((2, 2, 2, 2)),
            dma((3, 2, 2)),
            dma((4,)),
            dma((4, 3)),
            dma((4, 3)),
            dma((2,)),
            dma((2, 4)),
            dma((2,)),
            dma((4, 2, 2)),
            dma((2, 2, 2)),
            dma((2,)),
        ],
        compiler_params=pltpu.CompilerParams(
            collective_id=0, has_side_effects=True, vmem_limit_bytes=62 * 2**20
        ),
    )(
        token_ids,
        embed_table.reshape(4096, 8, 256),
        w_qkv.reshape(WIDTH, 512),
        w_out,
        gates,
        norm_gain.astype(F32).reshape(4, 1024),
        head_gain,
        gate_bias,
        owner,
    )
    block_out, memory_c, memory_n, memory_m = pl.pallas_call(
        tail,
        out_shape=(
            jax.ShapeDtypeStruct((2, ROWS, 256), BF16),
            jax.ShapeDtypeStruct((KEY, VAL), F32),
            jax.ShapeDtypeStruct((1, KEY), F32),
            jax.ShapeDtypeStruct((1, 1), F32),
        ),
        in_specs=[vmem, vmem, vmem],
        out_specs=(vmem, vmem, vmem, vmem),
    )(block_out, mem, aux)
    memory_c = memory_c[None, None, None]
    memory_n = memory_n[None, None]
    memory_m = memory_m[None]
    return (block_out, memory_c, memory_n, memory_m)


def solution(mesh):
    return jax.shard_map(
        local,
        mesh=mesh,
        in_specs=(
            P(None, "ctx"),
            P(None, "hr"),
            P(),
            P(None, "hr", None, None),
            P(),
            P(),
            P(),
            P(None, "hr"),
            P(),
        ),
        out_specs=(
            P(None, "ctx", "hr"),
            P("ctx", "hr", None, None, None),
            P("ctx", "hr", None, None),
            P("ctx", "hr", None),
        ),
        check_vma=False,
    )
```

```python
import jax
import jax.numpy as jnp
from jax import lax
from jax.experimental import pallas as pl
from jax.experimental.pallas import tpu as pltpu
from jax.sharding import PartitionSpec as P

MESH = pl.DeviceIdType.MESH
F32 = jnp.float32
BF16 = jnp.bfloat16
very_negative = -1e30
epsilon = 1e-06

WIDTH = 4096
ROWS = 1024
HALF = 512
PIECES = 4
PIECE = HALF // PIECES
KEY = 256
VAL = 512
SENDS = 192
SPREAD = 384
DIRECT = 512
TILE = 256


def dot(a, b):
    return jnp.dot(a, b, preferred_element_type=F32)


def dot_t(a, b):
    return lax.dot_general(a, b, (((1,), (1,)), ((), ())), preferred_element_type=F32)


def kernel(
    ids,
    table,
    w_own,
    w_out,
    w_gate,
    norm_gain,
    head_gain,
    bias,
    owner,
    out,
    out_mem,
    out_aux,
    tbl,
    emb,
    xb,
    wb,
    wo,
    qs,
    ks,
    vs,
    gs,
    scales,
    num,
    den,
    rows_in,
    cols_in,
    sum_c,
    sum_aux,
    pair_c,
    pair_aux,
    state_c,
    hn,
    act,
    own_p,
    total,
    rows_got,
    mem_got,
    aux_got,
    aux_out,
    send_sem,
    local_sem,
    sem_tbl,
    sem_a,
    sem_ring,
    sem_sib,
    sem_w,
    sem_wz,
    sem_wo,
    sem_woz,
    sem_wos,
    sem_mate,
    sem_pair,
    sem_hn,
    sem_act,
    sem_out,
    sem_mem,
):
    c = lax.axis_index("ctx")
    h = lax.axis_index("hr")
    x, y = h // 4, h % 4
    z, k = c // 2, c % 2
    req, par = y // 2, y % 2

    def dev(x_, y_, z_, k_):
        return (z_ * 2 + k_, x_ * 4 + y_)

    def rel(base, step):
        return lax.rem(base + step, 4)

    sib = dev(x, y, z, 1 - k)
    x_next, x_prev = dev(rel(x, 1), y, z, k), dev(rel(x, 3), y, z, k)
    y_next, y_prev = dev(x, rel(y, 1), z, k), dev(x, rel(y, 3), z, k)
    z_next, z_prev = dev(x, y, rel(z, 1), k), dev(x, y, rel(z, 3), k)
    mate = dev(x, 2 * req + 1 - par, z, k)

    copies = []
    for part in range(4):
        rows = pl.ds(part * 1024, 1024)
        copies.append(pltpu.make_async_copy(table.at[rows], tbl.at[rows], sem_tbl.at[part]))
        copies[-1].start()

    partners = [sib]
    for step in (1, 2, 3):
        for core in (0, 1):
            partners.append(dev(x, rel(y, step), z, core))
        partners.append(dev(rel(x, step), y, z, k))
        partners.append(dev(x, y, rel(z, step), k))
    barrier = pltpu.get_barrier_semaphore()
    for partner in partners:
        pl.semaphore_signal(barrier, inc=1, device_id=partner, device_id_type=MESH)
    pl.semaphore_wait(barrier, len(partners))

    pending = []

    def push(src, dst, sem, target, when=None):
        slot = len(pending)
        copy = pltpu.make_async_remote_copy(
            src_ref=src,
            dst_ref=dst,
            send_sem=send_sem.at[slot],
            recv_sem=sem,
            device_id=target,
            device_id_type=MESH,
        )
        pending.append((copy, when))
        if when is None:
            copy.start()
        else:
            pl.when(when)(copy.start)

    def here(src, dst, sem, when):
        copy = pltpu.make_async_copy(src, dst, sem)
        pl.when(when)(copy.start)

    def arrived(dst, sem, when=None):
        copy = pltpu.make_async_remote_copy(
            src_ref=dst,
            dst_ref=dst,
            send_sem=send_sem.at[0],
            recv_sem=sem,
            device_id=sib,
            device_id_type=MESH,
        )
        if when is None:
            copy.wait_recv()
        else:
            pl.when(when)(copy.wait_recv)

    k_half = k * HALF
    xl, xr, xo = rel(x, 3), rel(x, 1), rel(x, 2)
    zl, zr, zo = rel(z, 3), rel(z, 1), rel(z, 2)

    sub_tile = lax.broadcasted_iota(jnp.int32, (8, 256), 0)

    def look(r_, start):
        def body(step, carry):
            base = pl.multiple_of(start + step * 16, 16)
            eights = []
            for eight in (0, 1):
                found = jnp.zeros((8, 256), F32)
                for t in range(8):
                    token = ids[r_, base + eight * 8 + t]
                    turned = pltpu.roll(
                        tbl[lax.shift_right_logical(token, 3)].astype(F32),
                        lax.rem(t + 8 - lax.rem(token, 8), 8),
                        0,
                    )
                    found = jnp.where(sub_tile == t, turned, found)
                eights.append(found)
            emb[r_, pl.ds(base, 16), :] = jnp.concatenate(eights, axis=0).astype(BF16)
            return carry

        lax.fori_loop(0, PIECE // 16, body, 0)

    def look_and_send(piece):
        for r_ in (0, 1):
            for kd in (0, 1):
                y_to = 2 * r_ + k
                mine = (y_to == y) & (kd == k)
                start = kd * HALF + piece * PIECE
                look(r_, start)
                src = emb.at[r_, pl.ds(start, PIECE), :]
                dst = xb.at[x, piece, kd, :, pl.ds(pl.multiple_of(y * 256, 256), 256)]
                push(src, dst, sem_a.at[piece, y], dev(x, y_to, z, kd), jnp.logical_not(mine))
                here(src, dst, sem_a.at[piece, y], mine)

    w_local = pltpu.make_async_copy(w_own, wb.at[y % 2], local_sem.at[0])
    o_local = pltpu.make_async_copy(w_out, wo.at[y], local_sem.at[1])

    def rows_of(block, core, piece, half=None):
        if half is None:
            return xb.at[block, piece, core]
        return xb.at[block, piece, core, pl.ds(half * (PIECE // 2), PIECE // 2), :]

    def ring_start(piece):
        for y_ in range(4):
            arrived(
                xb.at[x, piece, k, :, pl.ds(y_ * 256, 256)],
                sem_a.at[piece, y_],
            )
        block = rows_of(x, k, piece)
        push(block, block, sem_ring.at[0, piece], x_next)
        push(block, block, sem_ring.at[1, piece], x_prev)
        push(block, block, sem_sib.at[0, piece], sib)

    def ring_middle(piece):
        block = rows_of(xl, k, piece)
        arrived(block, sem_ring.at[0, piece])
        half = rows_of(xl, k, piece, 0)
        push(half, half, sem_ring.at[2, piece], x_next)
        push(block, block, sem_sib.at[1, piece], sib)
        block = rows_of(xr, k, piece)
        arrived(block, sem_ring.at[1, piece])
        half = rows_of(xr, k, piece, 1)
        push(half, half, sem_ring.at[3, piece], x_prev)
        push(block, block, sem_sib.at[2, piece], sib)

    def ring_end(piece):
        for half in (0, 1):
            arrived(rows_of(xo, k, piece, half), sem_ring.at[2 + half, piece])
        block = rows_of(xo, k, piece)
        push(block, block, sem_sib.at[3, piece], sib)

    def w_part(late, kind, j, plane, part, half=None):
        if kind == 0:
            start, size = (plane * 2 + part) * SPREAD, SPREAD
        else:
            start, size = 8 * SPREAD + part * DIRECT, DIRECT
        if half is not None:
            start, size = start + half * (size // 2), size // 2
        if not isinstance(start, int):
            start = pl.multiple_of(start, 64)
        cols = slice(None)
        if j == 0:
            cols = pl.ds(0 if late else KEY, KEY)
        return (j, pl.ds(start, size), cols)

    def w_send(late, kind):
        core = y // 2
        for j in (0,) if late else (0, 1):
            at = w_part(late, kind, j, z, k)
            src = w_own.at[at[1], at[2]]
            mine = y % 2 == j
            push(src, wb.at[at], sem_w.at[late, kind, j, k, 0], dev(x, rel(y, 1), z, core), mine)
            push(src, wb.at[at], sem_w.at[late, kind, j, k, 0], dev(x, rel(y, 3), z, core), mine)

    away = [lax.rem(y - 2 * k - j + 4, 4) for j in (0, 1)]
    foreign = [step != 0 for step in away]

    def w_near(late, kind):
        for j in (0,) if late else (0, 1):
            near = (away[j] == 1) | (away[j] == 3)
            for part in (0, 1):
                sems = sem_w.at[late, kind, j, part]
                arrived(wb.at[w_part(late, kind, j, z, part)], sems.at[0], near)
                half = wb.at[w_part(late, kind, j, z, part, 0)]
                push(half, half, sems.at[0], y_next, away[j] == 1)
                half = wb.at[w_part(late, kind, j, z, part, 1)]
                push(half, half, sems.at[1], y_prev, away[j] == 3)
                if kind == 0:
                    w_along_z(late, j, part, near)

    def w_far(late, kind):
        for j in (0,) if late else (0, 1):
            far = away[j] == 2
            for part in (0, 1):
                for half in (0, 1):
                    arrived(
                        wb.at[w_part(late, kind, j, z, part, half)],
                        sem_w.at[late, kind, j, part, half],
                        far,
                    )
                if kind == 0:
                    w_along_z(late, j, part, far)

    def w_along_z(late, j, part, when):
        block = wb.at[w_part(late, 0, j, z, part)]
        push(block, block, sem_wz.at[late, 0, j, part], z_next, when)
        push(block, block, sem_wz.at[late, 1, j, part], z_prev, when)

    def w_middle(late):
        for j in (0,) if late else (0, 1):
            for part in (0, 1):
                from_left = wb.at[w_part(late, 0, j, zl, part)]
                from_right = wb.at[w_part(late, 0, j, zr, part)]
                arrived(from_left, sem_wz.at[late, 0, j, part], foreign[j])
                arrived(from_right, sem_wz.at[late, 1, j, part], foreign[j])
                if part == 0:
                    push(from_left, from_left, sem_wz.at[late, 2, j, 0], z_next, foreign[j])
                else:
                    push(from_right, from_right, sem_wz.at[late, 2, j, 1], z_prev, foreign[j])

    def w_end(late):
        for j in (0,) if late else (0, 1):
            for part in (0, 1):
                arrived(
                    wb.at[w_part(late, 0, j, zo, part)], sem_wz.at[late, 2, j, part], foreign[j]
                )

    def o_part(y_, plane, core, half=None):
        start, size = plane * 1024 + core * 512, 512
        if half is not None:
            start, size = start + half * 256, 256
        return wo.at[y_, pl.ds(pl.multiple_of(start, 256), size), :]

    def o_send():
        for step in (1, 3, 2):
            push(
                w_out.at[pl.ds(pl.multiple_of(z * 1024 + k * 512, 512), 512), :],
                o_part(y, z, k),
                sem_wo.at[y],
                dev(x, rel(y, step), z, k),
            )

    others = [rel(y, step) for step in (1, 2, 3)]

    def o_along_z():
        for index, y_ in enumerate(others):
            block = o_part(y_, z, k)
            arrived(block, sem_wo.at[y_])
            push(block, block, sem_woz.at[0, index], z_next)
            push(block, block, sem_woz.at[1, index], z_prev)
            push(block, block, sem_wos.at[0, index], sib)

    def norm(block, piece, scale):
        wide = xb[block, piece].astype(F32).reshape(2 * PIECE, 1024)
        return (wide * scale * norm_gain[block : block + 1, :]).astype(BF16)

    def spread(target, piece, value):
        for core in (0, 1):
            start = core * HALF + piece * PIECE
            target[start : start + PIECE, :] = value[core * PIECE : (core + 1) * PIECE, :]

    def project(piece):
        for index, block_x in enumerate((x, xl, xr, xo)):
            arrived(rows_of(block_x, 1 - k, piece), sem_sib.at[index, piece])
        squares = jnp.zeros((2 * PIECE, 1), F32)
        for block in range(4):
            wide = xb[block, piece].astype(F32).reshape(2 * PIECE, 1024)
            squares += jnp.sum(wide * wide, axis=1, keepdims=True)
        scale = lax.rsqrt(squares / WIDTH + epsilon)
        scales[piece] = jnp.broadcast_to(scale, (2 * PIECE, 128))
        keys, values = jnp.zeros((2 * PIECE, KEY), F32), jnp.zeros((2 * PIECE, VAL), F32)
        gate = jnp.zeros((16, 2 * PIECE), F32)
        for block in range(4):
            depth = slice(block * 1024, block * 1024 + 1024)
            normed = norm(block, piece, scale)
            keys = keys + dot(normed, wb[0, depth, KEY:])
            values = values + dot(normed, wb[1, depth, :])
            gate = gate + dot_t(w_gate[:, depth], normed)
        spread(ks, piece, keys.astype(BF16))
        spread(vs, piece, values.astype(BF16))
        for core in (0, 1):
            start = core * HALF + piece * PIECE
            gs[:, start : start + PIECE] = gate[:, core * PIECE : (core + 1) * PIECE]

    def project_queries(piece):
        scale = scales[piece][:, 0:1]
        queries = jnp.zeros((2 * PIECE, KEY), F32)
        for block in range(4):
            normed = norm(block, piece, scale)
            queries = queries + dot(normed, wb[0, block * 1024 : block * 1024 + 1024, :KEY])
        spread(qs, piece, queries.astype(BF16))

    w_send(0, 0)
    for copy in copies:
        copy.wait()
    pl.when(k == y // 2)(w_local.start)
    o_local.start()
    look_and_send(0)
    look_and_send(1)
    w_near(0, 0)
    look_and_send(2)
    ring_start(0)
    look_and_send(3)
    w_far(0, 0)
    w_send(0, 1)
    ring_start(1)
    ring_start(2)
    ring_middle(0)
    ring_start(3)
    ring_middle(1)
    w_near(0, 1)
    w_send(1, 0)
    w_send(1, 1)
    w_middle(0)
    ring_middle(2)
    ring_end(0)
    ring_middle(3)
    ring_end(1)
    w_far(0, 1)
    o_send()
    w_near(1, 0)
    w_near(1, 1)
    pl.when(k == y // 2)(w_local.wait)
    w_end(0)
    project(0)
    ring_end(2)
    project(1)
    w_far(1, 0)
    ring_end(3)
    project(2)
    project(3)
    w_middle(1)
    w_far(1, 1)
    o_along_z()

    head = 2 * x + k
    gates = gs[...]
    sub = lax.broadcasted_iota(jnp.int32, (16, ROWS), 0)
    gate_in = jnp.sum(jnp.where(sub == head, gates, 0.0), axis=0, keepdims=True)
    pre_forget = jnp.sum(jnp.where(sub == head + 8, gates, 0.0), axis=0, keepdims=True)
    gate_in = jnp.broadcast_to(gate_in, (8, ROWS)) + bias[0, head]
    pre_forget = jnp.broadcast_to(pre_forget, (8, ROWS)) + bias[1, head]
    log_forget = jnp.minimum(pre_forget, 0.0) - jnp.log1p(jnp.exp(-jnp.abs(pre_forget)))
    lane = lax.broadcasted_iota(jnp.int32, (8, ROWS), 1)
    cum = log_forget
    step = 1
    while step < ROWS:
        cum = cum + jnp.where(lane >= step, pltpu.roll(cum, step, 1), 0.0)
        step *= 2
    lead = gate_in - cum
    peak = lead
    step = 1
    while step < ROWS:
        peak = jnp.maximum(peak, jnp.where(lane >= step, pltpu.roll(peak, step, 1), very_negative))
        step *= 2
    rows_in[0:8, :] = cum
    rows_in[8:16, :] = lead
    rows_in[16:24, :] = peak
    last_peak = jnp.max(lead, axis=1, keepdims=True)[0:1, :]
    decay = jnp.sum(jnp.where(lane == ROWS - 1, cum, 0.0), axis=1, keepdims=True)[0:1, :]
    rows_in[24:32, :] = jnp.exp(lead - last_peak)
    rows_in[32:, :] = jnp.zeros((96, ROWS), F32)
    cols_in[...] = rows_in[...].T

    scaled = ks[...].astype(F32) * cols_in[:, 24:25]
    norm_sum = jnp.sum(scaled, axis=0, keepdims=True)
    memory = lax.dot_general(
        scaled.astype(BF16), vs[...], (((0,), (0,)), ((), ())), preferred_element_type=F32
    )
    sum_c[par] = memory.astype(BF16)
    row = lax.broadcasted_iota(jnp.int32, (8, KEY), 0)
    sum_aux[par] = jnp.where(row == 0, norm_sum, jnp.where(row == 1, decay + last_peak, decay))
    push(sum_aux.at[par], sum_aux.at[par], sem_mate.at[0], mate)
    push(sum_c.at[par], sum_c.at[par], sem_mate.at[1], mate)

    w_end(1)
    for piece in range(PIECES):
        project_queries(piece)

    lead_row = rows_in[8:9, :]

    def within(index):
        rows = slice(index * TILE, (index + 1) * TILE)
        seen = (index + 1) * TILE
        scores = dot_t(qs[rows, :], ks[:seen, :])
        t_at = lax.broadcasted_iota(jnp.int32, (TILE, seen), 0) + index * TILE
        s_at = lax.broadcasted_iota(jnp.int32, (TILE, seen), 1)
        exponent = jnp.where(t_at >= s_at, lead_row[:, :seen] - cols_in[rows, 16:17], very_negative)
        weighted = jnp.exp(exponent) * (scores * 0.0625)
        num[rows, :] = dot(weighted.astype(BF16), vs[:seen, :])
        den[rows, :] = jnp.broadcast_to(jnp.sum(weighted, axis=1, keepdims=True), (TILE, 128))

    def twice(value):
        return jnp.concatenate([value, value], axis=1)

    def join(state, c_ref, aux_ref, at):
        decay_, top, norm = state
        later = aux_ref[at]
        peak_, falls = later[1:2, :], later[2:3, :]
        joined = jnp.maximum(falls + top, peak_)
        one, two = jnp.exp(falls + top - joined), jnp.exp(peak_ - joined)
        state_c[...] = twice(one) * state_c[...] + twice(two) * c_ref[at].astype(F32)
        return decay_ + falls, joined, one * norm + two * later[0:1, :]

    def start_state():
        state_c[...] = jnp.zeros_like(state_c)
        zero = jnp.zeros((1, KEY), F32)
        return zero, jnp.full((1, KEY), very_negative, F32), zero

    other = 1 - par
    arrived(sum_aux.at[other], sem_mate.at[0])
    arrived(sum_c.at[other], sem_mate.at[1])
    state = start_state()
    for at in (0, 1):
        state = join(state, sum_c, sum_aux, at)
    pair_c[z] = state_c[...].astype(BF16)
    pair_aux[z] = jnp.where(row == 0, state[2], jnp.where(row == 1, state[1], state[0]))
    for step in (1, 3, 2):
        to = dev(x, y, rel(z, step), k)
        push(pair_aux.at[z], pair_aux.at[z], sem_pair.at[0, z], to)
        push(pair_c.at[z], pair_c.at[z], sem_pair.at[1, z], to)
    for index in range(4):
        within(index)

    for step in (1, 3, 2):
        z_ = rel(z, step)
        arrived(pair_aux.at[z_], sem_pair.at[0, z_])
        arrived(pair_c.at[z_], sem_pair.at[1, z_])

    for index, y_ in enumerate(others):
        from_left, from_right = o_part(y_, zl, k), o_part(y_, zr, k)
        arrived(from_left, sem_woz.at[0, index])
        arrived(from_right, sem_woz.at[1, index])
        half = o_part(y_, zl, k, 0)
        push(half, half, sem_woz.at[2, index], z_next)
        half = o_part(y_, zr, k, 1)
        push(half, half, sem_woz.at[3, index], z_prev)

    def pairs(limit):
        return lax.fori_loop(
            0, limit, lambda at, state: join(state, pair_c, pair_aux, at), start_state()
        )

    state = pairs(z)
    _, top_in, norm_in = lax.fori_loop(
        0, par, lambda at, state: join(state, sum_c, sum_aux, at), state
    )
    sub8 = lax.broadcasted_iota(jnp.int32, (8, VAL), 0)
    gain = jnp.sum(
        jnp.where(sub8 == head, head_gain[...].astype(F32), 0.0), axis=0, keepdims=True
    )
    memory_in = state_c[...].astype(BF16)

    def finish(start):
        rows = pl.ds(pl.multiple_of(start, TILE), TILE)
        q = qs[rows, :]
        carried = dot(q, memory_in) * 0.0625
        carried_norm = jnp.sum(q.astype(F32) * norm_in, axis=1, keepdims=True) * 0.0625
        columns = cols_in[rows, :]
        here_max = columns[:, 16:17]
        both = jnp.maximum(top_in[:, 0:1], here_max)
        inner, outer = jnp.exp(here_max - both), jnp.exp(top_in[:, 0:1] - both)
        row_max = columns[:, 0:1] + both
        bottom = inner * den[rows, :][:, 0:1] + outer * carried_norm
        divisor = jnp.maximum(jnp.abs(bottom), jnp.exp(-row_max))
        hidden = (inner * num[rows, :] + outer * carried) / divisor
        scale = lax.rsqrt(jnp.mean(hidden * hidden, axis=1, keepdims=True) + epsilon)
        return (hidden * scale * gain).astype(BF16)

    def act_of(block, kk, tile, half=None):
        start, size = tile * TILE, TILE
        if half is not None:
            start, size = start + half * (TILE // 2), TILE // 2
        return act.at[block, kk, pl.ds(start, size), :]

    def act_start(kk, order, tile):
        block = act_of(x, kk, tile)
        push(block, block, sem_act.at[0, order, tile], x_next)
        push(block, block, sem_act.at[1, order, tile], x_prev)

    for tile in (0, 1):
        act[x, k, tile * TILE : (tile + 1) * TILE, :] = finish(k_half + tile * TILE)
        act_start(k, 0, tile)
    for tile in (0, 1):
        rows = slice(tile * TILE, (tile + 1) * TILE)
        hn[rows, :] = finish((1 - k) * HALF + tile * TILE)
        push(hn.at[rows, :], act_of(x, k, tile), sem_hn.at[tile], sib)
    for tile in (0, 1):
        arrived(act_of(x, 1 - k, tile), sem_hn.at[tile])
        act_start(1 - k, 1, tile)

    for index, y_ in enumerate(others):
        block = o_part(y_, zl, k)
        push(block, block, sem_wos.at[1, index], sib)
        block = o_part(y_, zr, k)
        push(block, block, sem_wos.at[2, index], sib)
        arrived(o_part(y_, zo, k, 0), sem_woz.at[2, index])
        arrived(o_part(y_, zo, k, 1), sem_woz.at[3, index])
        block = o_part(y_, zo, k)
        push(block, block, sem_wos.at[3, index], sib)

    for order, kk in ((0, k), (1, 1 - k)):
        for tile in (0, 1):
            arrived(act_of(xl, kk, tile), sem_act.at[0, order, tile])
            half = act_of(xl, kk, tile, 0)
            push(half, half, sem_act.at[2, order, tile], x_next)
            arrived(act_of(xr, kk, tile), sem_act.at[1, order, tile])
            half = act_of(xr, kk, tile, 1)
            push(half, half, sem_act.at[3, order, tile], x_prev)

    _, top_end, norm_end = pairs(4)
    aux_out[...] = jnp.where(row == 0, norm_end, top_end)
    keep_here = (k == req) & (par == k)
    mem_to = dev(x, 2 * k + req, z, par)
    push(state_c, mem_got, sem_mem.at[0], mem_to, jnp.logical_not(keep_here))
    push(aux_out, aux_got, sem_mem.at[1], mem_to, jnp.logical_not(keep_here))
    here(state_c, mem_got, sem_mem.at[0], keep_here)
    here(aux_out, aux_got, sem_mem.at[1], keep_here)

    o_local.wait()
    for index, y_ in enumerate(others):
        for at, plane in enumerate((z, zl, zr, zo)):
            arrived(o_part(y_, plane, 1 - k), sem_wos.at[at, index])

    def mixed(block, tile, y_):
        rows = slice(tile * TILE, (tile + 1) * TILE)
        start = pl.multiple_of(block * 1024, 1024)
        return dot(act[block, 0, rows, :], wo[y_, pl.ds(start, 512), :]) + dot(
            act[block, 1, rows, :], wo[y_, pl.ds(start + 512, 512), :]
        )

    for tile in (0, 1):
        for y_ in range(4):
            own_p[tile * TILE : (tile + 1) * TILE, y_ * 256 : y_ * 256 + 256] = (
                mixed(x, tile, y_) + mixed(xl, tile, y_) + mixed(xr, tile, y_)
            )
    for tile in (0, 1):
        rows = slice(tile * TILE, (tile + 1) * TILE)
        for order, kk in ((0, k), (1, 1 - k)):
            for half in (0, 1):
                arrived(act_of(xo, kk, tile, half), sem_act.at[2 + half, order, tile])
        for y_ in range(4):
            cols = slice(y_ * 256, y_ * 256 + 256)
            total[rows, cols] = (own_p[rows, cols] + mixed(xo, tile, y_)).astype(BF16)
            src = total.at[rows, cols]
            dst = rows_got.at[req, pl.ds(pl.multiple_of(k_half + tile * TILE, TILE), TILE), :]
            mine = (y == y_) & (par == k)
            push(src, dst, sem_out.at[tile, req, k], dev(x, y_, z, par), jnp.logical_not(mine))
            here(src, dst, sem_out.at[tile, req, k], mine)

    arrived(mem_got, sem_mem.at[0])
    arrived(aux_got, sem_mem.at[1])
    keep = jnp.where(owner[h] == c, 1.0, 0.0)
    out_mem[...] = mem_got[...] * keep
    out_aux[...] = aux_got[...] * keep
    for tile in (0, 1):
        for r_ in (0, 1):
            for k_ in (0, 1):
                rows = slice(k_ * HALF + tile * TILE, k_ * HALF + (tile + 1) * TILE)
                arrived(rows_got.at[r_, rows, :], sem_out.at[tile, r_, k_])
                out[r_, rows, :] = (
                    emb[r_, rows, :].astype(F32) + rows_got[r_, rows, :].astype(F32)
                ).astype(BF16)
    for copy, when in pending:
        if when is None:
            copy.wait_send()
        else:
            pl.when(when)(copy.wait_send)


def tail(rows, mem, aux, out, out_c, out_n, out_m):
    out[...] = rows[...]
    out_c[...] = mem[...]
    out_n[...] = aux[0:1, :]
    out_m[...] = aux[1:2, 0:1]


def local(token_ids, embed_table, norm_gain, w_qkv, w_gate, gate_bias, head_gain, w_out, owner):
    gates = jnp.transpose(w_gate, (1, 2, 0)).reshape(16, WIDTH)
    vmem = pl.BlockSpec(memory_space=pltpu.VMEM)
    smem = pl.BlockSpec(memory_space=pltpu.SMEM)
    hbm = pl.BlockSpec(memory_space=pl.ANY)
    dma = pltpu.SemaphoreType.DMA
    block_out, mem, aux = pl.pallas_call(
        kernel,
        out_shape=(
            jax.ShapeDtypeStruct((2, ROWS, 256), BF16),
            jax.ShapeDtypeStruct((KEY, VAL), F32),
            jax.ShapeDtypeStruct((8, KEY), F32),
        ),
        in_specs=[smem, hbm, hbm, hbm, vmem, vmem, vmem, smem, smem],
        out_specs=(vmem, vmem, vmem),
        scratch_shapes=[
            pltpu.VMEM((4096, 8, 256), BF16),
            pltpu.VMEM((2, ROWS, 256), BF16),
            pltpu.VMEM((4, PIECES, 2, PIECE, 1024), BF16),
            pltpu.VMEM((2, WIDTH, 512), BF16),
            pltpu.VMEM((4, WIDTH, 256), BF16),
            pltpu.VMEM((ROWS, KEY), BF16),
            pltpu.VMEM((ROWS, KEY), BF16),
            pltpu.VMEM((ROWS, VAL), BF16),
            pltpu.VMEM((16, ROWS), F32),
            pltpu.VMEM((PIECES, 2 * PIECE, 128), F32),
            pltpu.VMEM((ROWS, VAL), F32),
            pltpu.VMEM((ROWS, 128), F32),
            pltpu.VMEM((128, ROWS), F32),
            pltpu.VMEM((ROWS, 128), F32),
            pltpu.VMEM((2, KEY, VAL), BF16),
            pltpu.VMEM((2, 8, KEY), F32),
            pltpu.VMEM((4, KEY, VAL), BF16),
            pltpu.VMEM((4, 8, KEY), F32),
            pltpu.VMEM((KEY, VAL), F32),
            pltpu.VMEM((HALF, VAL), BF16),
            pltpu.VMEM((4, 2, HALF, VAL), BF16),
            pltpu.VMEM((HALF, 1024), F32),
            pltpu.VMEM((HALF, 1024), BF16),
            pltpu.VMEM((2, ROWS, 256), BF16),
            pltpu.VMEM((KEY, VAL), F32),
            pltpu.VMEM((8, KEY), F32),
            pltpu.VMEM((8, KEY), F32),
            dma((SENDS,)),
            dma((2,)),
            dma((4,)),
            dma((PIECES, 4)),
            dma((4, PIECES)),
            dma((4, PIECES)),
            dma((2, 2, 2, 2, 2)),
            dma((2, 3, 2, 2)),
            dma((4,)),
            dma((4, 3)),
            dma((4, 3)),
            dma((2,)),
            dma((2, 4)),
            dma((2,)),
            dma((4, 2, 2)),
            dma((2, 2, 2)),
            dma((2,)),
        ],
        compiler_params=pltpu.CompilerParams(
            collective_id=0, has_side_effects=True, vmem_limit_bytes=62 * 2**20
        ),
    )(
        token_ids,
        embed_table.reshape(4096, 8, 256),
        w_qkv.reshape(WIDTH, 512),
        w_out,
        gates,
        norm_gain.astype(F32).reshape(4, 1024),
        head_gain,
        gate_bias,
        owner,
    )
    block_out, memory_c, memory_n, memory_m = pl.pallas_call(
        tail,
        out_shape=(
            jax.ShapeDtypeStruct((2, ROWS, 256), BF16),
            jax.ShapeDtypeStruct((KEY, VAL), F32),
            jax.ShapeDtypeStruct((1, KEY), F32),
            jax.ShapeDtypeStruct((1, 1), F32),
        ),
        in_specs=[vmem, vmem, vmem],
        out_specs=(vmem, vmem, vmem, vmem),
    )(block_out, mem, aux)
    memory_c = memory_c[None, None, None]
    memory_n = memory_n[None, None]
    memory_m = memory_m[None]
    return (block_out, memory_c, memory_n, memory_m)


def solution(mesh):
    return jax.shard_map(
        local,
        mesh=mesh,
        in_specs=(
            P(None, "ctx"),
            P(None, "hr"),
            P(),
            P(None, "hr", None, None),
            P(),
            P(),
            P(),
            P(None, "hr"),
            P(),
        ),
        out_specs=(
            P(None, "ctx", "hr"),
            P("ctx", "hr", None, None, None),
            P("ctx", "hr", None, None),
            P("ctx", "hr", None),
        ),
        check_vma=False,
    )
```

```python
import jax
import jax.numpy as jnp
from jax import lax
from jax.experimental import pallas as pl
from jax.experimental.pallas import tpu as pltpu
from jax.sharding import PartitionSpec as P

MESH = pl.DeviceIdType.MESH
F32 = jnp.float32
BF16 = jnp.bfloat16
very_negative = -1e30
epsilon = 1e-06

WIDTH = 4096
ROWS = 1024
HALF = 512
PIECES = 4
PIECE = HALF // PIECES
KEY = 256
VAL = 512
SENDS = 192
SPREAD = 320
DIRECT = 768
O_SPREAD = 256
O_DIRECT = 1024
TILE = 256


def dot(a, b):
    return jnp.dot(a, b, preferred_element_type=F32)


def dot_t(a, b):
    return lax.dot_general(a, b, (((1,), (1,)), ((), ())), preferred_element_type=F32)


def kernel(
    ids,
    table,
    w_own,
    w_out,
    w_gate,
    norm_gain,
    head_gain,
    bias,
    owner,
    out,
    out_mem,
    out_aux,
    tbl,
    emb,
    xb,
    wb,
    wo,
    qs,
    ks,
    vs,
    gs,
    scales,
    num,
    den,
    rows_in,
    cols_in,
    sum_c,
    sum_aux,
    pair_c,
    pair_aux,
    state_c,
    hn,
    act,
    own_p,
    total,
    rows_got,
    mem_out,
    mem_got,
    aux_got,
    aux_out,
    send_sem,
    local_sem,
    sem_tbl,
    sem_a,
    sem_ring,
    sem_sib,
    sem_w,
    sem_wz,
    sem_wo,
    sem_woz,
    sem_wos,
    sem_mate,
    sem_pair,
    sem_hn,
    sem_act,
    sem_out,
    sem_mem,
):
    c = lax.axis_index("ctx")
    h = lax.axis_index("hr")
    x, y = h // 4, h % 4
    z, k = c // 2, c % 2
    req, par = y // 2, y % 2

    def dev(x_, y_, z_, k_):
        return (z_ * 2 + k_, x_ * 4 + y_)

    def rel(base, step):
        return lax.rem(base + step, 4)

    sib = dev(x, y, z, 1 - k)
    x_next, x_prev = dev(rel(x, 1), y, z, k), dev(rel(x, 3), y, z, k)
    y_next, y_prev = dev(x, rel(y, 1), z, k), dev(x, rel(y, 3), z, k)
    z_next, z_prev = dev(x, y, rel(z, 1), k), dev(x, y, rel(z, 3), k)
    mate = dev(x, 2 * req + 1 - par, z, k)

    copies = []
    for part in range(4):
        rows = pl.ds(part * 1024, 1024)
        copies.append(pltpu.make_async_copy(table.at[rows], tbl.at[rows], sem_tbl.at[part]))
        copies[-1].start()

    partners = [sib]
    for step in (1, 2, 3):
        for core in (0, 1):
            partners.append(dev(x, rel(y, step), z, core))
        partners.append(dev(rel(x, step), y, z, k))
        partners.append(dev(x, y, rel(z, step), k))
    barrier = pltpu.get_barrier_semaphore()
    for partner in partners:
        pl.semaphore_signal(barrier, inc=1, device_id=partner, device_id_type=MESH)
    pl.semaphore_wait(barrier, len(partners))

    pending = []

    def push(src, dst, sem, target, when=None):
        slot = len(pending)
        copy = pltpu.make_async_remote_copy(
            src_ref=src,
            dst_ref=dst,
            send_sem=send_sem.at[slot],
            recv_sem=sem,
            device_id=target,
            device_id_type=MESH,
        )
        pending.append((copy, when))
        if when is None:
            copy.start()
        else:
            pl.when(when)(copy.start)

    def here(src, dst, sem, when):
        copy = pltpu.make_async_copy(src, dst, sem)
        pl.when(when)(copy.start)

    def arrived(dst, sem, when=None):
        copy = pltpu.make_async_remote_copy(
            src_ref=dst,
            dst_ref=dst,
            send_sem=send_sem.at[0],
            recv_sem=sem,
            device_id=sib,
            device_id_type=MESH,
        )
        if when is None:
            copy.wait_recv()
        else:
            pl.when(when)(copy.wait_recv)

    k_half = k * HALF
    xl, xr, xo = rel(x, 3), rel(x, 1), rel(x, 2)
    zl, zr, zo = rel(z, 3), rel(z, 1), rel(z, 2)

    sub_tile = lax.broadcasted_iota(jnp.int32, (8, 256), 0)

    def look(r_, start):
        def body(step, carry):
            base = pl.multiple_of(start + step * 16, 16)
            eights = []
            for eight in (0, 1):
                found = jnp.zeros((8, 256), F32)
                for t in range(8):
                    token = ids[r_, base + eight * 8 + t]
                    turned = pltpu.roll(
                        tbl[lax.shift_right_logical(token, 3)].astype(F32),
                        lax.rem(t + 8 - lax.rem(token, 8), 8),
                        0,
                    )
                    found = jnp.where(sub_tile == t, turned, found)
                eights.append(found)
            emb[r_, pl.ds(base, 16), :] = jnp.concatenate(eights, axis=0).astype(BF16)
            return carry

        lax.fori_loop(0, PIECE // 16, body, 0)

    def look_and_send(piece):
        for r_ in (0, 1):
            for kd in (0, 1):
                y_to = 2 * r_ + k
                mine = (y_to == y) & (kd == k)
                start = kd * HALF + piece * PIECE
                look(r_, start)
                src = emb.at[r_, pl.ds(start, PIECE), :]
                dst = xb.at[x, piece, kd, :, pl.ds(pl.multiple_of(y * 256, 256), 256)]
                push(src, dst, sem_a.at[piece, y], dev(x, y_to, z, kd), jnp.logical_not(mine))
                here(src, dst, sem_a.at[piece, y], mine)

    w_local = pltpu.make_async_copy(w_own, wb.at[y % 2], local_sem.at[0])
    o_local = pltpu.make_async_copy(w_out, wo.at[y], local_sem.at[1])

    def rows_of(block, core, piece, half=None):
        if half is None:
            return xb.at[block, piece, core]
        return xb.at[block, piece, core, pl.ds(half * (PIECE // 2), PIECE // 2), :]

    def ring_start(piece):
        for y_ in range(4):
            arrived(
                xb.at[x, piece, k, :, pl.ds(y_ * 256, 256)],
                sem_a.at[piece, y_],
            )
        block = rows_of(x, k, piece)
        push(block, block, sem_ring.at[0, piece], x_next)
        push(block, block, sem_ring.at[1, piece], x_prev)
        push(block, block, sem_sib.at[0, piece], sib)

    def ring_middle(piece):
        block = rows_of(xl, k, piece)
        arrived(block, sem_ring.at[0, piece])
        half = rows_of(xl, k, piece, 0)
        push(half, half, sem_ring.at[2, piece], x_next)
        push(block, block, sem_sib.at[1, piece], sib)
        block = rows_of(xr, k, piece)
        arrived(block, sem_ring.at[1, piece])
        half = rows_of(xr, k, piece, 1)
        push(half, half, sem_ring.at[3, piece], x_prev)
        push(block, block, sem_sib.at[2, piece], sib)

    def ring_end(piece):
        for half in (0, 1):
            arrived(rows_of(xo, k, piece, half), sem_ring.at[2 + half, piece])
        block = rows_of(xo, k, piece)
        push(block, block, sem_sib.at[3, piece], sib)

    def w_part(kind, j, plane, part, half=None):
        if kind == 0:
            start, size = (plane * 2 + part) * SPREAD, SPREAD
        else:
            start, size = 8 * SPREAD + part * DIRECT, DIRECT
        if half is not None:
            start, size = start + half * (size // 2), size // 2
        if not isinstance(start, int):
            start = pl.multiple_of(start, 32)
        return (j, pl.ds(start, size), slice(None))

    def w_send(kind):
        core = y // 2
        at = w_part(kind, y % 2, z, k)
        src = w_own.at[at[1], at[2]]
        push(src, wb.at[at], sem_w.at[kind, y % 2, k, 0], dev(x, rel(y, 1), z, core))
        push(src, wb.at[at], sem_w.at[kind, y % 2, k, 0], dev(x, rel(y, 3), z, core))

    away = [lax.rem(y - 2 * k - j + 4, 4) for j in (0, 1)]
    foreign = [step != 0 for step in away]

    def w_near(kind):
        for j in (0, 1):
            near = (away[j] == 1) | (away[j] == 3)
            for part in (0, 1):
                sems = sem_w.at[kind, j, part]
                arrived(wb.at[w_part(kind, j, z, part)], sems.at[0], near)
                half = wb.at[w_part(kind, j, z, part, 0)]
                push(half, half, sems.at[0], y_next, away[j] == 1)
                half = wb.at[w_part(kind, j, z, part, 1)]
                push(half, half, sems.at[1], y_prev, away[j] == 3)
                if kind == 0:
                    w_along_z(j, part, near)

    def w_far(kind):
        for j in (0, 1):
            far = away[j] == 2
            for part in (0, 1):
                for half in (0, 1):
                    arrived(
                        wb.at[w_part(kind, j, z, part, half)],
                        sem_w.at[kind, j, part, half],
                        far,
                    )
                if kind == 0:
                    w_along_z(j, part, far)

    def w_along_z(j, part, when):
        block = wb.at[w_part(0, j, z, part)]
        push(block, block, sem_wz.at[0, j, part], z_next, when)
        push(block, block, sem_wz.at[1, j, part], z_prev, when)

    def w_middle():
        for j in (0, 1):
            for part in (0, 1):
                from_left = wb.at[w_part(0, j, zl, part)]
                from_right = wb.at[w_part(0, j, zr, part)]
                arrived(from_left, sem_wz.at[0, j, part], foreign[j])
                arrived(from_right, sem_wz.at[1, j, part], foreign[j])
                if part == 0:
                    push(from_left, from_left, sem_wz.at[2, j, 0], z_next, foreign[j])
                else:
                    push(from_right, from_right, sem_wz.at[2, j, 1], z_prev, foreign[j])

    def w_end():
        for j in (0, 1):
            for part in (0, 1):
                arrived(
                    wb.at[w_part(0, j, zo, part)], sem_wz.at[2, j, part], foreign[j]
                )

    def o_part(kind, y_, plane, core, half=None):
        if kind == 0:
            start, size = (plane * 2 + core) * O_SPREAD, O_SPREAD
        else:
            start, size = 8 * O_SPREAD + core * O_DIRECT, O_DIRECT
        if half is not None:
            start, size = start + half * (size // 2), size // 2
        return (y_, pl.ds(pl.multiple_of(start, 64), size), slice(None))

    others = [rel(y, step) for step in (1, 2, 3)]

    def o_send(kind):
        at = o_part(kind, y, z, k)
        for step in (1, 3, 2):
            push(w_out.at[at[1], :], wo.at[at], sem_wo.at[kind, y], dev(x, rel(y, step), z, k))

    def o_got(kind):
        for index, y_ in enumerate(others):
            block = wo.at[o_part(kind, y_, z, k)]
            arrived(block, sem_wo.at[kind, y_])
            if kind == 0:
                push(block, block, sem_woz.at[0, index], z_next)
                push(block, block, sem_woz.at[1, index], z_prev)
            push(block, block, sem_wos.at[4 * kind, index], sib)

    def o_middle():
        for index, y_ in enumerate(others):
            block = wo.at[o_part(0, y_, zl, k)]
            arrived(block, sem_woz.at[0, index])
            half = wo.at[o_part(0, y_, zl, k, 0)]
            push(half, half, sem_woz.at[2, index], z_next)
            push(block, block, sem_wos.at[1, index], sib)
            block = wo.at[o_part(0, y_, zr, k)]
            arrived(block, sem_woz.at[1, index])
            half = wo.at[o_part(0, y_, zr, k, 1)]
            push(half, half, sem_woz.at[3, index], z_prev)
            push(block, block, sem_wos.at[2, index], sib)

    def o_end():
        for index, y_ in enumerate(others):
            arrived(wo.at[o_part(0, y_, zo, k, 0)], sem_woz.at[2, index])
            arrived(wo.at[o_part(0, y_, zo, k, 1)], sem_woz.at[3, index])
            block = wo.at[o_part(0, y_, zo, k)]
            push(block, block, sem_wos.at[3, index], sib)

    def o_wait():
        o_local.wait()
        for index, y_ in enumerate(others):
            for at, plane in enumerate((z, zl, zr, zo)):
                arrived(wo.at[o_part(0, y_, plane, 1 - k)], sem_wos.at[at, index])
            arrived(wo.at[o_part(1, y_, z, 1 - k)], sem_wos.at[4, index])

    def norm(block, piece, scale):
        wide = xb[block, piece].astype(F32).reshape(2 * PIECE, 1024)
        return (wide * scale * norm_gain[block : block + 1, :]).astype(BF16)

    def spread(target, piece, value):
        for core in (0, 1):
            start = core * HALF + piece * PIECE
            target[start : start + PIECE, :] = value[core * PIECE : (core + 1) * PIECE, :]

    def project(piece):
        for index, block_x in enumerate((x, xl, xr, xo)):
            arrived(rows_of(block_x, 1 - k, piece), sem_sib.at[index, piece])
        squares = jnp.zeros((2 * PIECE, 1), F32)
        for block in range(4):
            wide = xb[block, piece].astype(F32).reshape(2 * PIECE, 1024)
            squares += jnp.sum(wide * wide, axis=1, keepdims=True)
        scale = lax.rsqrt(squares / WIDTH + epsilon)
        scales[piece] = jnp.broadcast_to(scale, (2 * PIECE, 128))
        keys, values = jnp.zeros((2 * PIECE, KEY), F32), jnp.zeros((2 * PIECE, VAL), F32)
        gate = jnp.zeros((16, 2 * PIECE), F32)
        for block in range(4):
            depth = slice(block * 1024, block * 1024 + 1024)
            normed = norm(block, piece, scale)
            keys = keys + dot(normed, wb[0, depth, KEY:])
            values = values + dot(normed, wb[1, depth, :])
            gate = gate + dot_t(w_gate[:, depth], normed)
        spread(ks, piece, keys.astype(BF16))
        spread(vs, piece, values.astype(BF16))
        for core in (0, 1):
            start = core * HALF + piece * PIECE
            gs[:, start : start + PIECE] = gate[:, core * PIECE : (core + 1) * PIECE]

    def project_queries(piece):
        scale = scales[piece][:, 0:1]
        queries = jnp.zeros((2 * PIECE, KEY), F32)
        for block in range(4):
            normed = norm(block, piece, scale)
            queries = queries + dot(normed, wb[0, block * 1024 : block * 1024 + 1024, :KEY])
        spread(qs, piece, queries.astype(BF16))

    w_send(0)
    for copy in copies:
        copy.wait()
    pl.when(k == y // 2)(w_local.start)
    o_local.start()
    look_and_send(0)
    look_and_send(1)
    w_near(0)
    look_and_send(2)
    ring_start(0)
    look_and_send(3)
    w_far(0)
    w_send(1)
    ring_start(1)
    ring_start(2)
    ring_middle(0)
    ring_start(3)
    ring_middle(1)
    w_near(1)
    w_middle()
    ring_middle(2)
    ring_end(0)
    ring_middle(3)
    ring_end(1)
    w_far(1)
    pl.when(k == y // 2)(w_local.wait)
    w_end()
    project(0)
    ring_end(2)
    project(1)
    ring_end(3)
    project(2)
    project(3)

    head = 2 * x + k
    gates = gs[...]
    sub = lax.broadcasted_iota(jnp.int32, (16, ROWS), 0)
    gate_in = jnp.sum(jnp.where(sub == head, gates, 0.0), axis=0, keepdims=True)
    pre_forget = jnp.sum(jnp.where(sub == head + 8, gates, 0.0), axis=0, keepdims=True)
    gate_in = jnp.broadcast_to(gate_in, (8, ROWS)) + bias[0, head]
    pre_forget = jnp.broadcast_to(pre_forget, (8, ROWS)) + bias[1, head]
    log_forget = jnp.minimum(pre_forget, 0.0) - jnp.log1p(jnp.exp(-jnp.abs(pre_forget)))
    lane = lax.broadcasted_iota(jnp.int32, (8, ROWS), 1)
    cum = log_forget
    step = 1
    while step < ROWS:
        cum = cum + jnp.where(lane >= step, pltpu.roll(cum, step, 1), 0.0)
        step *= 2
    lead = gate_in - cum
    peak = lead
    step = 1
    while step < ROWS:
        peak = jnp.maximum(peak, jnp.where(lane >= step, pltpu.roll(peak, step, 1), very_negative))
        step *= 2
    rows_in[0:8, :] = cum
    rows_in[8:16, :] = lead
    rows_in[16:24, :] = peak
    last_peak = jnp.max(lead, axis=1, keepdims=True)[0:1, :]
    decay = jnp.sum(jnp.where(lane == ROWS - 1, cum, 0.0), axis=1, keepdims=True)[0:1, :]
    rows_in[24:32, :] = jnp.exp(lead - last_peak)
    rows_in[32:, :] = jnp.zeros((96, ROWS), F32)
    cols_in[...] = rows_in[...].T

    scaled = ks[...].astype(F32) * cols_in[:, 24:25]
    norm_sum = jnp.sum(scaled, axis=0, keepdims=True)
    memory = lax.dot_general(
        scaled.astype(BF16), vs[...], (((0,), (0,)), ((), ())), preferred_element_type=F32
    )
    sum_c[par] = memory.astype(BF16)
    row = lax.broadcasted_iota(jnp.int32, (8, KEY), 0)
    sum_aux[par] = jnp.where(row == 0, norm_sum, jnp.where(row == 1, decay + last_peak, decay))
    push(sum_aux.at[par], sum_aux.at[par], sem_mate.at[0], mate)
    push(sum_c.at[par], sum_c.at[par], sem_mate.at[1], mate)

    o_send(0)

    lead_row = rows_in[8:9, :]

    def within(index):
        rows = slice(index * TILE, (index + 1) * TILE)
        seen = (index + 1) * TILE
        scores = dot_t(qs[rows, :], ks[:seen, :])
        t_at = lax.broadcasted_iota(jnp.int32, (TILE, seen), 0) + index * TILE
        s_at = lax.broadcasted_iota(jnp.int32, (TILE, seen), 1)
        exponent = jnp.where(t_at >= s_at, lead_row[:, :seen] - cols_in[rows, 16:17], very_negative)
        weighted = jnp.exp(exponent) * (scores * 0.0625)
        num[rows, :] = dot(weighted.astype(BF16), vs[:seen, :])
        den[rows, :] = jnp.broadcast_to(jnp.sum(weighted, axis=1, keepdims=True), (TILE, 128))

    def twice(value):
        return jnp.concatenate([value, value], axis=1)

    def join(state, c_ref, aux_ref, at):
        decay_, top, norm = state
        later = aux_ref[at]
        peak_, falls = later[1:2, :], later[2:3, :]
        joined = jnp.maximum(falls + top, peak_)
        one, two = jnp.exp(falls + top - joined), jnp.exp(peak_ - joined)
        state_c[...] = twice(one) * state_c[...] + twice(two) * c_ref[at].astype(F32)
        return decay_ + falls, joined, one * norm + two * later[0:1, :]

    def start_state():
        state_c[...] = jnp.zeros_like(state_c)
        zero = jnp.zeros((1, KEY), F32)
        return zero, jnp.full((1, KEY), very_negative, F32), zero

    other = 1 - par
    arrived(sum_aux.at[other], sem_mate.at[0])
    arrived(sum_c.at[other], sem_mate.at[1])
    state = start_state()
    for at in (0, 1):
        state = join(state, sum_c, sum_aux, at)
    pair_c[z] = state_c[...].astype(BF16)
    pair_aux[z] = jnp.where(row == 0, state[2], jnp.where(row == 1, state[1], state[0]))
    for step in (1, 3, 2):
        to = dev(x, y, rel(z, step), k)
        push(pair_aux.at[z], pair_aux.at[z], sem_pair.at[0, z], to)
        push(pair_c.at[z], pair_c.at[z], sem_pair.at[1, z], to)
    o_send(1)
    for piece in range(PIECES):
        project_queries(piece)
    for index in range(4):
        within(index)

    for step in (1, 3, 2):
        z_ = rel(z, step)
        arrived(pair_aux.at[z_], sem_pair.at[0, z_])
        arrived(pair_c.at[z_], sem_pair.at[1, z_])

    o_got(0)

    def pairs(limit):
        return lax.fori_loop(
            0, limit, lambda at, state: join(state, pair_c, pair_aux, at), start_state()
        )

    state = pairs(z)
    _, top_in, norm_in = lax.fori_loop(
        0, par, lambda at, state: join(state, sum_c, sum_aux, at), state
    )
    sub8 = lax.broadcasted_iota(jnp.int32, (8, VAL), 0)
    gain = jnp.sum(
        jnp.where(sub8 == head, head_gain[...].astype(F32), 0.0), axis=0, keepdims=True
    )
    memory_in = state_c[...].astype(BF16)

    def finish(start):
        rows = pl.ds(pl.multiple_of(start, PIECE), PIECE)
        q = qs[rows, :]
        carried = dot(q, memory_in) * 0.0625
        carried_norm = jnp.sum(q.astype(F32) * norm_in, axis=1, keepdims=True) * 0.0625
        columns = cols_in[rows, :]
        here_max = columns[:, 16:17]
        both = jnp.maximum(top_in[:, 0:1], here_max)
        inner, outer = jnp.exp(here_max - both), jnp.exp(top_in[:, 0:1] - both)
        row_max = columns[:, 0:1] + both
        bottom = inner * den[rows, :][:, 0:1] + outer * carried_norm
        divisor = jnp.maximum(jnp.abs(bottom), jnp.exp(-row_max))
        hidden = (inner * num[rows, :] + outer * carried) / divisor
        scale = lax.rsqrt(jnp.mean(hidden * hidden, axis=1, keepdims=True) + epsilon)
        return (hidden * scale * gain).astype(BF16)

    def act_start(tile):
        arrived(act.at[x, tile, 1 - k], sem_hn.at[tile])
        block = act.at[x, tile]
        push(block, block, sem_act.at[0, tile], x_next)
        push(block, block, sem_act.at[1, tile], x_prev)

    def act_middle(tile):
        arrived(act.at[xl, tile], sem_act.at[0, tile])
        push(act.at[xl, tile, 0], act.at[xl, tile, 0], sem_act.at[2, tile], x_next)
        arrived(act.at[xr, tile], sem_act.at[1, tile])
        push(act.at[xr, tile, 1], act.at[xr, tile, 1], sem_act.at[3, tile], x_prev)

    for tile in range(PIECES):
        hn[tile] = finish((1 - k) * HALF + tile * PIECE)
        push(hn.at[tile], act.at[x, tile, k], sem_hn.at[tile], sib)
        act[x, tile, k] = finish(k_half + tile * PIECE)
        if tile > 0:
            act_start(tile - 1)
    act_start(PIECES - 1)
    act_middle(0)
    act_middle(1)
    o_middle()
    act_middle(2)
    o_got(1)
    act_middle(3)

    _, top_end, norm_end = pairs(4)
    aux_out[...] = jnp.where(row == 0, norm_end, top_end)
    keep_here = (k == req) & (par == k)
    mem_to = dev(x, 2 * k + req, z, par)
    mem_out[...] = state_c[...].astype(BF16)
    push(mem_out, mem_got, sem_mem.at[0], mem_to, jnp.logical_not(keep_here))
    push(aux_out, aux_got, sem_mem.at[1], mem_to, jnp.logical_not(keep_here))
    here(mem_out, mem_got, sem_mem.at[0], keep_here)
    here(aux_out, aux_got, sem_mem.at[1], keep_here)

    o_end()
    o_wait()

    def mixed(block, tiles, y_):
        start = pl.multiple_of(block * 1024, 1024)
        first = act[block, tiles, 0].reshape(-1, VAL)
        second = act[block, tiles, 1].reshape(-1, VAL)
        return dot(first, wo[y_, pl.ds(start, 512), :]) + dot(
            second, wo[y_, pl.ds(start + 512, 512), :]
        )

    for half in (0, 1):
        tiles = pl.ds(half * 2, 2)
        for y_ in range(4):
            own_p[half * TILE : (half + 1) * TILE, y_ * 256 : y_ * 256 + 256] = (
                mixed(x, tiles, y_) + mixed(xl, tiles, y_) + mixed(xr, tiles, y_)
            )
    for tile in range(PIECES):
        rows = slice(tile * PIECE, (tile + 1) * PIECE)
        arrived(act.at[xo, tile, 0], sem_act.at[2, tile])
        arrived(act.at[xo, tile, 1], sem_act.at[3, tile])
        for y_ in range(4):
            cols = slice(y_ * 256, y_ * 256 + 256)
            value = own_p[rows, cols] + mixed(xo, pl.ds(tile, 1), y_)
            total[rows, cols] = value.astype(BF16)
            src = total.at[rows, cols]
            dst = rows_got.at[req, pl.ds(pl.multiple_of(k_half + tile * PIECE, PIECE), PIECE), :]
            mine = (y == y_) & (par == k)
            push(src, dst, sem_out.at[tile, req, k], dev(x, y_, z, par), jnp.logical_not(mine))
            here(src, dst, sem_out.at[tile, req, k], mine)

    arrived(mem_got, sem_mem.at[0])
    arrived(aux_got, sem_mem.at[1])
    keep = jnp.where(owner[h] == c, 1.0, 0.0)
    out_mem[...] = mem_got[...].astype(F32) * keep
    out_aux[...] = aux_got[...] * keep
    for tile in range(PIECES):
        for r_ in (0, 1):
            for k_ in (0, 1):
                rows = slice(k_ * HALF + tile * PIECE, k_ * HALF + (tile + 1) * PIECE)
                arrived(rows_got.at[r_, rows, :], sem_out.at[tile, r_, k_])
                out[r_, rows, :] = (
                    emb[r_, rows, :].astype(F32) + rows_got[r_, rows, :].astype(F32)
                ).astype(BF16)
    for copy, when in pending:
        if when is None:
            copy.wait_send()
        else:
            pl.when(when)(copy.wait_send)


def tail(rows, mem, aux, out, out_c, out_n, out_m):
    out[...] = rows[...]
    out_c[...] = mem[...]
    out_n[...] = aux[0:1, :]
    out_m[...] = aux[1:2, 0:1]


def local(token_ids, embed_table, norm_gain, w_qkv, w_gate, gate_bias, head_gain, w_out, owner):
    gates = jnp.transpose(w_gate, (1, 2, 0)).reshape(16, WIDTH)
    vmem = pl.BlockSpec(memory_space=pltpu.VMEM)
    smem = pl.BlockSpec(memory_space=pltpu.SMEM)
    hbm = pl.BlockSpec(memory_space=pl.ANY)
    dma = pltpu.SemaphoreType.DMA
    block_out, mem, aux = pl.pallas_call(
        kernel,
        out_shape=(
            jax.ShapeDtypeStruct((2, ROWS, 256), BF16),
            jax.ShapeDtypeStruct((KEY, VAL), F32),
            jax.ShapeDtypeStruct((8, KEY), F32),
        ),
        in_specs=[smem, hbm, hbm, hbm, vmem, vmem, vmem, smem, smem],
        out_specs=(vmem, vmem, vmem),
        scratch_shapes=[
            pltpu.VMEM((4096, 8, 256), BF16),
            pltpu.VMEM((2, ROWS, 256), BF16),
            pltpu.VMEM((4, PIECES, 2, PIECE, 1024), BF16),
            pltpu.VMEM((2, WIDTH, 512), BF16),
            pltpu.VMEM((4, WIDTH, 256), BF16),
            pltpu.VMEM((ROWS, KEY), BF16),
            pltpu.VMEM((ROWS, KEY), BF16),
            pltpu.VMEM((ROWS, VAL), BF16),
            pltpu.VMEM((16, ROWS), F32),
            pltpu.VMEM((PIECES, 2 * PIECE, 128), F32),
            pltpu.VMEM((ROWS, VAL), F32),
            pltpu.VMEM((ROWS, 128), F32),
            pltpu.VMEM((128, ROWS), F32),
            pltpu.VMEM((ROWS, 128), F32),
            pltpu.VMEM((2, KEY, VAL), BF16),
            pltpu.VMEM((2, 8, KEY), F32),
            pltpu.VMEM((4, KEY, VAL), BF16),
            pltpu.VMEM((4, 8, KEY), F32),
            pltpu.VMEM((KEY, VAL), F32),
            pltpu.VMEM((PIECES, PIECE, VAL), BF16),
            pltpu.VMEM((4, PIECES, 2, PIECE, VAL), BF16),
            pltpu.VMEM((HALF, 1024), F32),
            pltpu.VMEM((HALF, 1024), BF16),
            pltpu.VMEM((2, ROWS, 256), BF16),
            pltpu.VMEM((KEY, VAL), BF16),
            pltpu.VMEM((KEY, VAL), BF16),
            pltpu.VMEM((8, KEY), F32),
            pltpu.VMEM((8, KEY), F32),
            dma((SENDS,)),
            dma((2,)),
            dma((4,)),
            dma((PIECES, 4)),
            dma((4, PIECES)),
            dma((4, PIECES)),
            dma((2, 2, 2, 2)),
            dma((3, 2, 2)),
            dma((2, 4)),
            dma((4, 3)),
            dma((5, 3)),
            dma((2,)),
            dma((2, 4)),
            dma((PIECES,)),
            dma((4, PIECES)),
            dma((PIECES, 2, 2)),
            dma((2,)),
        ],
        compiler_params=pltpu.CompilerParams(
            collective_id=0, has_side_effects=True, vmem_limit_bytes=62 * 2**20
        ),
    )(
        token_ids,
        embed_table.reshape(4096, 8, 256),
        w_qkv.reshape(WIDTH, 512),
        w_out,
        gates,
        norm_gain.astype(F32).reshape(4, 1024),
        head_gain,
        gate_bias,
        owner,
    )
    block_out, memory_c, memory_n, memory_m = pl.pallas_call(
        tail,
        out_shape=(
            jax.ShapeDtypeStruct((2, ROWS, 256), BF16),
            jax.ShapeDtypeStruct((KEY, VAL), F32),
            jax.ShapeDtypeStruct((1, KEY), F32),
            jax.ShapeDtypeStruct((1, 1), F32),
        ),
        in_specs=[vmem, vmem, vmem],
        out_specs=(vmem, vmem, vmem, vmem),
    )(block_out, mem, aux)
    memory_c = memory_c[None, None, None]
    memory_n = memory_n[None, None]
    memory_m = memory_m[None]
    return (block_out, memory_c, memory_n, memory_m)


def solution(mesh):
    return jax.shard_map(
        local,
        mesh=mesh,
        in_specs=(
            P(None, "ctx"),
            P(None, "hr"),
            P(),
            P(None, "hr", None, None),
            P(),
            P(),
            P(),
            P(None, "hr"),
            P(),
        ),
        out_specs=(
            P(None, "ctx", "hr"),
            P("ctx", "hr", None, None, None),
            P("ctx", "hr", None, None),
            P("ctx", "hr", None),
        ),
        check_vma=False,
    )
```

```python
import jax
import jax.numpy as jnp
from jax import lax
from jax.experimental import pallas as pl
from jax.experimental.pallas import tpu as pltpu
from jax.sharding import PartitionSpec as P

MESH = pl.DeviceIdType.MESH
F32 = jnp.float32
BF16 = jnp.bfloat16
very_negative = -1e30
epsilon = 1e-06

WIDTH = 4096
ROWS = 1024
HALF = 512
PIECES = 4
PIECE = HALF // PIECES
KEY = 256
VAL = 512
SENDS = 192
SPREAD = 384
DIRECT = 512
O_SPREAD = 256
O_DIRECT = 1024
TILE = 256


def dot(a, b):
    return jnp.dot(a, b, preferred_element_type=F32)


def dot_t(a, b):
    return lax.dot_general(a, b, (((1,), (1,)), ((), ())), preferred_element_type=F32)


def kernel(
    ids,
    table,
    w_own,
    w_out,
    w_gate,
    norm_gain,
    head_gain,
    bias,
    owner,
    out,
    out_mem,
    out_aux,
    tbl,
    emb,
    xb,
    wb,
    wo,
    qs,
    ks,
    vs,
    gs,
    scales,
    num,
    den,
    rows_in,
    cols_in,
    sum_c,
    sum_aux,
    pair_c,
    pair_aux,
    state_c,
    hn,
    act,
    own_p,
    total,
    rows_got,
    mem_out,
    mem_got,
    aux_got,
    aux_out,
    send_sem,
    local_sem,
    sem_tbl,
    sem_a,
    sem_ring,
    sem_sib,
    sem_w,
    sem_wz,
    sem_wo,
    sem_woz,
    sem_wos,
    sem_mate,
    sem_pair,
    sem_hn,
    sem_act,
    sem_out,
    sem_mem,
):
    c = lax.axis_index("ctx")
    h = lax.axis_index("hr")
    x, y = h // 4, h % 4
    z, k = c // 2, c % 2
    req, par = y // 2, y % 2

    def dev(x_, y_, z_, k_):
        return (z_ * 2 + k_, x_ * 4 + y_)

    def rel(base, step):
        return lax.rem(base + step, 4)

    sib = dev(x, y, z, 1 - k)
    x_next, x_prev = dev(rel(x, 1), y, z, k), dev(rel(x, 3), y, z, k)
    y_next, y_prev = dev(x, rel(y, 1), z, k), dev(x, rel(y, 3), z, k)
    z_next, z_prev = dev(x, y, rel(z, 1), k), dev(x, y, rel(z, 3), k)
    mate = dev(x, 2 * req + 1 - par, z, k)

    copies = []
    for part in range(4):
        rows = pl.ds(part * 1024, 1024)
        copies.append(pltpu.make_async_copy(table.at[rows], tbl.at[rows], sem_tbl.at[part]))
        copies[-1].start()

    partners = [sib]
    for step in (1, 2, 3):
        for core in (0, 1):
            partners.append(dev(x, rel(y, step), z, core))
        partners.append(dev(rel(x, step), y, z, k))
        partners.append(dev(x, y, rel(z, step), k))
    barrier = pltpu.get_barrier_semaphore()
    for partner in partners:
        pl.semaphore_signal(barrier, inc=1, device_id=partner, device_id_type=MESH)
    pl.semaphore_wait(barrier, len(partners))

    pending = []

    def push(src, dst, sem, target, when=None):
        slot = len(pending)
        copy = pltpu.make_async_remote_copy(
            src_ref=src,
            dst_ref=dst,
            send_sem=send_sem.at[slot],
            recv_sem=sem,
            device_id=target,
            device_id_type=MESH,
        )
        pending.append((copy, when))
        if when is None:
            copy.start()
        else:
            pl.when(when)(copy.start)

    def here(src, dst, sem, when):
        copy = pltpu.make_async_copy(src, dst, sem)
        pl.when(when)(copy.start)

    def arrived(dst, sem, when=None):
        copy = pltpu.make_async_remote_copy(
            src_ref=dst,
            dst_ref=dst,
            send_sem=send_sem.at[0],
            recv_sem=sem,
            device_id=sib,
            device_id_type=MESH,
        )
        if when is None:
            copy.wait_recv()
        else:
            pl.when(when)(copy.wait_recv)

    k_half = k * HALF
    xl, xr, xo = rel(x, 3), rel(x, 1), rel(x, 2)
    zl, zr, zo = rel(z, 3), rel(z, 1), rel(z, 2)

    sub_tile = lax.broadcasted_iota(jnp.int32, (8, 256), 0)

    def look(r_, start):
        def body(step, carry):
            base = pl.multiple_of(start + step * 16, 16)
            eights = []
            for eight in (0, 1):
                found = jnp.zeros((8, 256), F32)
                for t in range(8):
                    token = ids[r_, base + eight * 8 + t]
                    turned = pltpu.roll(
                        tbl[lax.shift_right_logical(token, 3)].astype(F32),
                        lax.rem(t + 8 - lax.rem(token, 8), 8),
                        0,
                    )
                    found = jnp.where(sub_tile == t, turned, found)
                eights.append(found)
            emb[r_, pl.ds(base, 16), :] = jnp.concatenate(eights, axis=0).astype(BF16)
            return carry

        lax.fori_loop(0, PIECE // 16, body, 0)

    def look_and_send(piece):
        for r_ in (0, 1):
            for kd in (0, 1):
                y_to = 2 * r_ + k
                mine = (y_to == y) & (kd == k)
                start = kd * HALF + piece * PIECE
                look(r_, start)
                src = emb.at[r_, pl.ds(start, PIECE), :]
                dst = xb.at[x, piece, kd, :, pl.ds(pl.multiple_of(y * 256, 256), 256)]
                push(src, dst, sem_a.at[piece, y], dev(x, y_to, z, kd), jnp.logical_not(mine))
                here(src, dst, sem_a.at[piece, y], mine)

    w_local = pltpu.make_async_copy(w_own, wb.at[y % 2], local_sem.at[0])
    o_local = pltpu.make_async_copy(w_out, wo.at[y], local_sem.at[1])

    def rows_of(block, core, piece, half=None):
        if half is None:
            return xb.at[block, piece, core]
        return xb.at[block, piece, core, pl.ds(half * (PIECE // 2), PIECE // 2), :]

    def ring_start(piece):
        for y_ in range(4):
            arrived(
                xb.at[x, piece, k, :, pl.ds(y_ * 256, 256)],
                sem_a.at[piece, y_],
            )
        block = rows_of(x, k, piece)
        push(block, block, sem_ring.at[0, piece], x_next)
        push(block, block, sem_ring.at[1, piece], x_prev)
        push(block, block, sem_sib.at[0, piece], sib)

    def ring_middle(piece):
        block = rows_of(xl, k, piece)
        arrived(block, sem_ring.at[0, piece])
        half = rows_of(xl, k, piece, 0)
        push(half, half, sem_ring.at[2, piece], x_next)
        push(block, block, sem_sib.at[1, piece], sib)
        block = rows_of(xr, k, piece)
        arrived(block, sem_ring.at[1, piece])
        half = rows_of(xr, k, piece, 1)
        push(half, half, sem_ring.at[3, piece], x_prev)
        push(block, block, sem_sib.at[2, piece], sib)

    def ring_end(piece):
        for half in (0, 1):
            arrived(rows_of(xo, k, piece, half), sem_ring.at[2 + half, piece])
        block = rows_of(xo, k, piece)
        push(block, block, sem_sib.at[3, piece], sib)

    def w_part(kind, j, plane, part, half=None):
        if kind == 0:
            start, size = (plane * 2 + part) * SPREAD, SPREAD
        else:
            start, size = 8 * SPREAD + part * DIRECT, DIRECT
        if half is not None:
            start, size = start + half * (size // 2), size // 2
        if not isinstance(start, int):
            start = pl.multiple_of(start, 32)
        return (j, pl.ds(start, size), slice(None))

    def w_send(kind):
        core = y // 2
        at = w_part(kind, y % 2, z, k)
        src = w_own.at[at[1], at[2]]
        push(src, wb.at[at], sem_w.at[kind, y % 2, k, 0], dev(x, rel(y, 1), z, core))
        push(src, wb.at[at], sem_w.at[kind, y % 2, k, 0], dev(x, rel(y, 3), z, core))

    away = [lax.rem(y - 2 * k - j + 4, 4) for j in (0, 1)]
    foreign = [step != 0 for step in away]

    def w_near(kind):
        for j in (0, 1):
            near = (away[j] == 1) | (away[j] == 3)
            for part in (0, 1):
                sems = sem_w.at[kind, j, part]
                arrived(wb.at[w_part(kind, j, z, part)], sems.at[0], near)
                half = wb.at[w_part(kind, j, z, part, 0)]
                push(half, half, sems.at[0], y_next, away[j] == 1)
                half = wb.at[w_part(kind, j, z, part, 1)]
                push(half, half, sems.at[1], y_prev, away[j] == 3)
                if kind == 0:
                    w_along_z(j, part, near)

    def w_far(kind):
        for j in (0, 1):
            far = away[j] == 2
            for part in (0, 1):
                for half in (0, 1):
                    arrived(
                        wb.at[w_part(kind, j, z, part, half)],
                        sem_w.at[kind, j, part, half],
                        far,
                    )
                if kind == 0:
                    w_along_z(j, part, far)

    def w_along_z(j, part, when):
        block = wb.at[w_part(0, j, z, part)]
        push(block, block, sem_wz.at[0, j, part], z_next, when)
        push(block, block, sem_wz.at[1, j, part], z_prev, when)

    def w_middle():
        for j in (0, 1):
            for part in (0, 1):
                from_left = wb.at[w_part(0, j, zl, part)]
                from_right = wb.at[w_part(0, j, zr, part)]
                arrived(from_left, sem_wz.at[0, j, part], foreign[j])
                arrived(from_right, sem_wz.at[1, j, part], foreign[j])
                if part == 0:
                    push(from_left, from_left, sem_wz.at[2, j, 0], z_next, foreign[j])
                else:
                    push(from_right, from_right, sem_wz.at[2, j, 1], z_prev, foreign[j])

    def w_end():
        for j in (0, 1):
            for part in (0, 1):
                arrived(
                    wb.at[w_part(0, j, zo, part)], sem_wz.at[2, j, part], foreign[j]
                )

    def o_part(kind, y_, plane, core, half=None):
        if kind == 0:
            start, size = (plane * 2 + core) * O_SPREAD, O_SPREAD
        else:
            start, size = 8 * O_SPREAD + core * O_DIRECT, O_DIRECT
        if half is not None:
            start, size = start + half * (size // 2), size // 2
        return (y_, pl.ds(pl.multiple_of(start, 64), size), slice(None))

    others = [rel(y, step) for step in (1, 2, 3)]

    def o_send(kind):
        at = o_part(kind, y, z, k)
        for step in (1, 3, 2):
            push(w_out.at[at[1], :], wo.at[at], sem_wo.at[kind, y], dev(x, rel(y, step), z, k))

    def o_got(kind):
        for index, y_ in enumerate(others):
            block = wo.at[o_part(kind, y_, z, k)]
            arrived(block, sem_wo.at[kind, y_])
            if kind == 0:
                push(block, block, sem_woz.at[0, index], z_next)
                push(block, block, sem_woz.at[1, index], z_prev)
            push(block, block, sem_wos.at[4 * kind, index], sib)

    def o_middle():
        for index, y_ in enumerate(others):
            block = wo.at[o_part(0, y_, zl, k)]
            arrived(block, sem_woz.at[0, index])
            half = wo.at[o_part(0, y_, zl, k, 0)]
            push(half, half, sem_woz.at[2, index], z_next)
            push(block, block, sem_wos.at[1, index], sib)
            block = wo.at[o_part(0, y_, zr, k)]
            arrived(block, sem_woz.at[1, index])
            half = wo.at[o_part(0, y_, zr, k, 1)]
            push(half, half, sem_woz.at[3, index], z_prev)
            push(block, block, sem_wos.at[2, index], sib)

    def o_end():
        for index, y_ in enumerate(others):
            arrived(wo.at[o_part(0, y_, zo, k, 0)], sem_woz.at[2, index])
            arrived(wo.at[o_part(0, y_, zo, k, 1)], sem_woz.at[3, index])
            block = wo.at[o_part(0, y_, zo, k)]
            push(block, block, sem_wos.at[3, index], sib)

    def o_wait():
        o_local.wait()
        for index, y_ in enumerate(others):
            for at, plane in enumerate((z, zl, zr, zo)):
                arrived(wo.at[o_part(0, y_, plane, 1 - k)], sem_wos.at[at, index])
            arrived(wo.at[o_part(1, y_, z, 1 - k)], sem_wos.at[4, index])

    def norm(block, piece, scale):
        wide = xb[block, piece].astype(F32).reshape(2 * PIECE, 1024)
        return (wide * scale * norm_gain[block : block + 1, :]).astype(BF16)

    def spread(target, piece, value):
        for core in (0, 1):
            start = core * HALF + piece * PIECE
            target[start : start + PIECE, :] = value[core * PIECE : (core + 1) * PIECE, :]

    def prepare(piece):
        for index, block_x in enumerate((x, xl, xr, xo)):
            arrived(rows_of(block_x, 1 - k, piece), sem_sib.at[index, piece])
        squares = jnp.zeros((2 * PIECE, 1), F32)
        for block in range(4):
            wide = xb[block, piece].astype(F32).reshape(2 * PIECE, 1024)
            squares += jnp.sum(wide * wide, axis=1, keepdims=True)
        scale = lax.rsqrt(squares / WIDTH + epsilon)
        scales[piece] = jnp.broadcast_to(scale, (2 * PIECE, 128))

    def project(piece):
        scale = scales[piece][:, 0:1]
        keys, values = jnp.zeros((2 * PIECE, KEY), F32), jnp.zeros((2 * PIECE, VAL), F32)
        gate = jnp.zeros((16, 2 * PIECE), F32)
        for block in range(4):
            depth = slice(block * 1024, block * 1024 + 1024)
            normed = norm(block, piece, scale)
            keys = keys + dot(normed, wb[0, depth, KEY:])
            values = values + dot(normed, wb[1, depth, :])
            gate = gate + dot_t(w_gate[:, depth], normed)
        spread(ks, piece, keys.astype(BF16))
        spread(vs, piece, values.astype(BF16))
        for core in (0, 1):
            start = core * HALF + piece * PIECE
            gs[:, start : start + PIECE] = gate[:, core * PIECE : (core + 1) * PIECE]

    def project_queries(piece):
        scale = scales[piece][:, 0:1]
        queries = jnp.zeros((2 * PIECE, KEY), F32)
        for block in range(4):
            normed = norm(block, piece, scale)
            queries = queries + dot(normed, wb[0, block * 1024 : block * 1024 + 1024, :KEY])
        spread(qs, piece, queries.astype(BF16))

    w_send(0)
    for copy in copies:
        copy.wait()
    pl.when(k == y // 2)(w_local.start)
    o_local.start()
    look_and_send(0)
    look_and_send(1)
    w_near(0)
    look_and_send(2)
    ring_start(0)
    look_and_send(3)
    w_far(0)
    w_send(1)
    ring_start(1)
    ring_start(2)
    ring_middle(0)
    ring_start(3)
    ring_middle(1)
    w_middle()
    ring_middle(2)
    w_near(1)
    ring_end(0)
    ring_middle(3)
    ring_end(1)
    prepare(0)
    prepare(1)
    ring_end(2)
    prepare(2)
    w_far(1)
    pl.when(k == y // 2)(w_local.wait)
    w_end()
    project(0)
    project(1)
    ring_end(3)
    prepare(3)
    project(2)
    project(3)

    head = 2 * x + k
    gates = gs[...]
    sub = lax.broadcasted_iota(jnp.int32, (16, ROWS), 0)
    gate_in = jnp.sum(jnp.where(sub == head, gates, 0.0), axis=0, keepdims=True)
    pre_forget = jnp.sum(jnp.where(sub == head + 8, gates, 0.0), axis=0, keepdims=True)
    gate_in = jnp.broadcast_to(gate_in, (8, ROWS)) + bias[0, head]
    pre_forget = jnp.broadcast_to(pre_forget, (8, ROWS)) + bias[1, head]
    log_forget = jnp.minimum(pre_forget, 0.0) - jnp.log1p(jnp.exp(-jnp.abs(pre_forget)))
    lane = lax.broadcasted_iota(jnp.int32, (8, ROWS), 1)
    cum = log_forget
    step = 1
    while step < ROWS:
        cum = cum + jnp.where(lane >= step, pltpu.roll(cum, step, 1), 0.0)
        step *= 2
    lead = gate_in - cum
    peak = lead
    step = 1
    while step < ROWS:
        peak = jnp.maximum(peak, jnp.where(lane >= step, pltpu.roll(peak, step, 1), very_negative))
        step *= 2
    rows_in[0:8, :] = cum
    rows_in[8:16, :] = lead
    rows_in[16:24, :] = peak
    last_peak = jnp.max(lead, axis=1, keepdims=True)[0:1, :]
    decay = jnp.sum(jnp.where(lane == ROWS - 1, cum, 0.0), axis=1, keepdims=True)[0:1, :]
    rows_in[24:32, :] = jnp.exp(lead - last_peak)
    rows_in[32:, :] = jnp.zeros((96, ROWS), F32)
    cols_in[...] = rows_in[...].T

    scaled = ks[...].astype(F32) * cols_in[:, 24:25]
    norm_sum = jnp.sum(scaled, axis=0, keepdims=True)
    memory = lax.dot_general(
        scaled.astype(BF16), vs[...], (((0,), (0,)), ((), ())), preferred_element_type=F32
    )
    sum_c[par] = memory.astype(BF16)
    row = lax.broadcasted_iota(jnp.int32, (8, KEY), 0)
    sum_aux[par] = jnp.where(row == 0, norm_sum, jnp.where(row == 1, decay + last_peak, decay))
    push(sum_aux.at[par], sum_aux.at[par], sem_mate.at[0], mate)
    push(sum_c.at[par], sum_c.at[par], sem_mate.at[1], mate)

    o_send(0)

    lead_row = rows_in[8:9, :]

    def within(index):
        rows = slice(index * TILE, (index + 1) * TILE)
        seen = (index + 1) * TILE
        scores = dot_t(qs[rows, :], ks[:seen, :])
        t_at = lax.broadcasted_iota(jnp.int32, (TILE, seen), 0) + index * TILE
        s_at = lax.broadcasted_iota(jnp.int32, (TILE, seen), 1)
        exponent = jnp.where(t_at >= s_at, lead_row[:, :seen] - cols_in[rows, 16:17], very_negative)
        weighted = jnp.exp(exponent) * (scores * 0.0625)
        num[rows, :] = dot(weighted.astype(BF16), vs[:seen, :])
        den[rows, :] = jnp.broadcast_to(jnp.sum(weighted, axis=1, keepdims=True), (TILE, 128))

    def twice(value):
        return jnp.concatenate([value, value], axis=1)

    def join(state, c_ref, aux_ref, at):
        decay_, top, norm = state
        later = aux_ref[at]
        peak_, falls = later[1:2, :], later[2:3, :]
        joined = jnp.maximum(falls + top, peak_)
        one, two = jnp.exp(falls + top - joined), jnp.exp(peak_ - joined)
        state_c[...] = twice(one) * state_c[...] + twice(two) * c_ref[at].astype(F32)
        return decay_ + falls, joined, one * norm + two * later[0:1, :]

    def start_state():
        state_c[...] = jnp.zeros_like(state_c)
        zero = jnp.zeros((1, KEY), F32)
        return zero, jnp.full((1, KEY), very_negative, F32), zero

    other = 1 - par
    arrived(sum_aux.at[other], sem_mate.at[0])
    arrived(sum_c.at[other], sem_mate.at[1])
    state = start_state()
    for at in (0, 1):
        state = join(state, sum_c, sum_aux, at)
    pair_c[z] = state_c[...].astype(BF16)
    pair_aux[z] = jnp.where(row == 0, state[2], jnp.where(row == 1, state[1], state[0]))
    for step in (1, 3, 2):
        to = dev(x, y, rel(z, step), k)
        push(pair_aux.at[z], pair_aux.at[z], sem_pair.at[0, z], to)
        push(pair_c.at[z], pair_c.at[z], sem_pair.at[1, z], to)
    o_send(1)
    for piece in range(PIECES):
        project_queries(piece)
    for index in range(4):
        within(index)

    for step in (1, 3, 2):
        z_ = rel(z, step)
        arrived(pair_aux.at[z_], sem_pair.at[0, z_])
        arrived(pair_c.at[z_], sem_pair.at[1, z_])

    o_got(0)

    def pairs(limit):
        return lax.fori_loop(
            0, limit, lambda at, state: join(state, pair_c, pair_aux, at), start_state()
        )

    state = pairs(z)
    _, top_in, norm_in = lax.fori_loop(
        0, par, lambda at, state: join(state, sum_c, sum_aux, at), state
    )
    sub8 = lax.broadcasted_iota(jnp.int32, (8, VAL), 0)
    gain = jnp.sum(
        jnp.where(sub8 == head, head_gain[...].astype(F32), 0.0), axis=0, keepdims=True
    )
    memory_in = state_c[...].astype(BF16)

    def finish(start):
        rows = pl.ds(pl.multiple_of(start, PIECE), PIECE)
        q = qs[rows, :]
        carried = dot(q, memory_in) * 0.0625
        carried_norm = jnp.sum(q.astype(F32) * norm_in, axis=1, keepdims=True) * 0.0625
        columns = cols_in[rows, :]
        here_max = columns[:, 16:17]
        both = jnp.maximum(top_in[:, 0:1], here_max)
        inner, outer = jnp.exp(here_max - both), jnp.exp(top_in[:, 0:1] - both)
        row_max = columns[:, 0:1] + both
        bottom = inner * den[rows, :][:, 0:1] + outer * carried_norm
        divisor = jnp.maximum(jnp.abs(bottom), jnp.exp(-row_max))
        hidden = (inner * num[rows, :] + outer * carried) / divisor
        scale = lax.rsqrt(jnp.mean(hidden * hidden, axis=1, keepdims=True) + epsilon)
        return (hidden * scale * gain).astype(BF16)

    def act_start(tile):
        arrived(act.at[x, tile, 1 - k], sem_hn.at[tile])
        block = act.at[x, tile]
        push(block, block, sem_act.at[0, tile], x_next)
        push(block, block, sem_act.at[1, tile], x_prev)

    def act_middle(tile):
        arrived(act.at[xl, tile], sem_act.at[0, tile])
        push(act.at[xl, tile, 0], act.at[xl, tile, 0], sem_act.at[2, tile], x_next)
        arrived(act.at[xr, tile], sem_act.at[1, tile])
        push(act.at[xr, tile, 1], act.at[xr, tile, 1], sem_act.at[3, tile], x_prev)

    for tile in range(PIECES):
        hn[tile] = finish((1 - k) * HALF + tile * PIECE)
        push(hn.at[tile], act.at[x, tile, k], sem_hn.at[tile], sib)
        act[x, tile, k] = finish(k_half + tile * PIECE)
        if tile > 0:
            act_start(tile - 1)
    act_start(PIECES - 1)
    act_middle(0)
    act_middle(1)
    o_middle()
    act_middle(2)
    o_got(1)
    act_middle(3)

    _, top_end, norm_end = pairs(4)
    aux_out[...] = jnp.where(row == 0, norm_end, top_end)
    keep_here = (k == req) & (par == k)
    mem_to = dev(x, 2 * k + req, z, par)
    mem_out[...] = state_c[...].astype(BF16)
    push(mem_out, mem_got, sem_mem.at[0], mem_to, jnp.logical_not(keep_here))
    push(aux_out, aux_got, sem_mem.at[1], mem_to, jnp.logical_not(keep_here))
    here(mem_out, mem_got, sem_mem.at[0], keep_here)
    here(aux_out, aux_got, sem_mem.at[1], keep_here)

    o_end()
    o_wait()

    def mixed(block, tiles, y_):
        start = pl.multiple_of(block * 1024, 1024)
        first = act[block, tiles, 0].reshape(-1, VAL)
        second = act[block, tiles, 1].reshape(-1, VAL)
        return dot(first, wo[y_, pl.ds(start, 512), :]) + dot(
            second, wo[y_, pl.ds(start + 512, 512), :]
        )

    for half in (0, 1):
        tiles = pl.ds(half * 2, 2)
        for y_ in range(4):
            own_p[half * TILE : (half + 1) * TILE, y_ * 256 : y_ * 256 + 256] = (
                mixed(x, tiles, y_) + mixed(xl, tiles, y_) + mixed(xr, tiles, y_)
            )
    for tile in range(PIECES):
        rows = slice(tile * PIECE, (tile + 1) * PIECE)
        arrived(act.at[xo, tile, 0], sem_act.at[2, tile])
        arrived(act.at[xo, tile, 1], sem_act.at[3, tile])
        for y_ in range(4):
            cols = slice(y_ * 256, y_ * 256 + 256)
            value = own_p[rows, cols] + mixed(xo, pl.ds(tile, 1), y_)
            total[rows, cols] = value.astype(BF16)
            src = total.at[rows, cols]
            dst = rows_got.at[req, pl.ds(pl.multiple_of(k_half + tile * PIECE, PIECE), PIECE), :]
            mine = (y == y_) & (par == k)
            push(src, dst, sem_out.at[tile, req, k], dev(x, y_, z, par), jnp.logical_not(mine))
            here(src, dst, sem_out.at[tile, req, k], mine)

    arrived(mem_got, sem_mem.at[0])
    arrived(aux_got, sem_mem.at[1])
    keep = jnp.where(owner[h] == c, 1.0, 0.0)
    out_mem[...] = mem_got[...].astype(F32) * keep
    out_aux[...] = aux_got[...] * keep
    for tile in range(PIECES):
        for r_ in (0, 1):
            for k_ in (0, 1):
                rows = slice(k_ * HALF + tile * PIECE, k_ * HALF + (tile + 1) * PIECE)
                arrived(rows_got.at[r_, rows, :], sem_out.at[tile, r_, k_])
                out[r_, rows, :] = (
                    emb[r_, rows, :].astype(F32) + rows_got[r_, rows, :].astype(F32)
                ).astype(BF16)
    for copy, when in pending:
        if when is None:
            copy.wait_send()
        else:
            pl.when(when)(copy.wait_send)


def tail(rows, mem, aux, out, out_c, out_n, out_m):
    out[...] = rows[...]
    out_c[...] = mem[...]
    out_n[...] = aux[0:1, :]
    out_m[...] = aux[1:2, 0:1]


def local(token_ids, embed_table, norm_gain, w_qkv, w_gate, gate_bias, head_gain, w_out, owner):
    gates = jnp.transpose(w_gate, (1, 2, 0)).reshape(16, WIDTH)
    vmem = pl.BlockSpec(memory_space=pltpu.VMEM)
    smem = pl.BlockSpec(memory_space=pltpu.SMEM)
    hbm = pl.BlockSpec(memory_space=pl.ANY)
    dma = pltpu.SemaphoreType.DMA
    block_out, mem, aux = pl.pallas_call(
        kernel,
        out_shape=(
            jax.ShapeDtypeStruct((2, ROWS, 256), BF16),
            jax.ShapeDtypeStruct((KEY, VAL), F32),
            jax.ShapeDtypeStruct((8, KEY), F32),
        ),
        in_specs=[smem, hbm, hbm, hbm, vmem, vmem, vmem, smem, smem],
        out_specs=(vmem, vmem, vmem),
        scratch_shapes=[
            pltpu.VMEM((4096, 8, 256), BF16),
            pltpu.VMEM((2, ROWS, 256), BF16),
            pltpu.VMEM((4, PIECES, 2, PIECE, 1024), BF16),
            pltpu.VMEM((2, WIDTH, 512), BF16),
            pltpu.VMEM((4, WIDTH, 256), BF16),
            pltpu.VMEM((ROWS, KEY), BF16),
            pltpu.VMEM((ROWS, KEY), BF16),
            pltpu.VMEM((ROWS, VAL), BF16),
            pltpu.VMEM((16, ROWS), F32),
            pltpu.VMEM((PIECES, 2 * PIECE, 128), F32),
            pltpu.VMEM((ROWS, VAL), F32),
            pltpu.VMEM((ROWS, 128), F32),
            pltpu.VMEM((128, ROWS), F32),
            pltpu.VMEM((ROWS, 128), F32),
            pltpu.VMEM((2, KEY, VAL), BF16),
            pltpu.VMEM((2, 8, KEY), F32),
            pltpu.VMEM((4, KEY, VAL), BF16),
            pltpu.VMEM((4, 8, KEY), F32),
            pltpu.VMEM((KEY, VAL), F32),
            pltpu.VMEM((PIECES, PIECE, VAL), BF16),
            pltpu.VMEM((4, PIECES, 2, PIECE, VAL), BF16),
            pltpu.VMEM((HALF, 1024), F32),
            pltpu.VMEM((HALF, 1024), BF16),
            pltpu.VMEM((2, ROWS, 256), BF16),
            pltpu.VMEM((KEY, VAL), BF16),
            pltpu.VMEM((KEY, VAL), BF16),
            pltpu.VMEM((8, KEY), F32),
            pltpu.VMEM((8, KEY), F32),
            dma((SENDS,)),
            dma((2,)),
            dma((4,)),
            dma((PIECES, 4)),
            dma((4, PIECES)),
            dma((4, PIECES)),
            dma((2, 2, 2, 2)),
            dma((3, 2, 2)),
            dma((2, 4)),
            dma((4, 3)),
            dma((5, 3)),
            dma((2,)),
            dma((2, 4)),
            dma((PIECES,)),
            dma((4, PIECES)),
            dma((PIECES, 2, 2)),
            dma((2,)),
        ],
        compiler_params=pltpu.CompilerParams(
            collective_id=0, has_side_effects=True, vmem_limit_bytes=62 * 2**20
        ),
    )(
        token_ids,
        embed_table.reshape(4096, 8, 256),
        w_qkv.reshape(WIDTH, 512),
        w_out,
        gates,
        norm_gain.astype(F32).reshape(4, 1024),
        head_gain,
        gate_bias,
        owner,
    )
    block_out, memory_c, memory_n, memory_m = pl.pallas_call(
        tail,
        out_shape=(
            jax.ShapeDtypeStruct((2, ROWS, 256), BF16),
            jax.ShapeDtypeStruct((KEY, VAL), F32),
            jax.ShapeDtypeStruct((1, KEY), F32),
            jax.ShapeDtypeStruct((1, 1), F32),
        ),
        in_specs=[vmem, vmem, vmem],
        out_specs=(vmem, vmem, vmem, vmem),
    )(block_out, mem, aux)
    memory_c = memory_c[None, None, None]
    memory_n = memory_n[None, None]
    memory_m = memory_m[None]
    return (block_out, memory_c, memory_n, memory_m)


def solution(mesh):
    return jax.shard_map(
        local,
        mesh=mesh,
        in_specs=(
            P(None, "ctx"),
            P(None, "hr"),
            P(),
            P(None, "hr", None, None),
            P(),
            P(),
            P(),
            P(None, "hr"),
            P(),
        ),
        out_specs=(
            P(None, "ctx", "hr"),
            P("ctx", "hr", None, None, None),
            P("ctx", "hr", None, None),
            P("ctx", "hr", None),
        ),
        check_vma=False,
    )
```
